256 devices in a mesh: row: 32 (over z, y), col: 8 (over x, core).
Axes of the slice: x: 4, y: 4, z: 8, core: 2. Of those that a mesh axis runs over, the one named last changes fastest.
Arguments:
- eigvecs: float32 [106496, 2048], P('row', 'col'), may hold values from -6 to 6
- reflect_y: float32 [8, 832, 64, 128], P(None, 'row'), may hold values from -0.5 to 0.5
- reflect_w: float32 [8, 832, 64, 128], P(None, 'row'), may hold values from -0.1875 to 0.1875
- panel_v: float32 [106496, 512], P('row', 'col'), may hold values from -0.01953125 to 0.01953125
- panel_t: float32 [2, 256, 256], replicated, may hold values from -0.1 to 1.8, as said below
Outputs:
- full_vectors: float32 [106496, 2048], P('row', 'col')
The draws below stay inside these ranges and needn't reach their ends.
Inputs may be any that keep to these rules, and one draw needn't show every extreme that they name: Each panel_t[p] is upper triangular; its diagonal lies between 0.2 and 1.8.
All inputs are finite; a program needn't handle non-finite values.
Results may differ from the reference program's by a relative error of at most 0.0001.
Values sent between devices are 32-bit elements; how exact they have to be, the bound alone decides.
No kernel may reach another device: no remote copies, remote signals or barrier semaphores. Data moves between devices by JAX's collectives and lax.ppermute only.
A program may use at most 128 MiB of HBM per device.

```python
import jax
import jax.numpy as jnp
from jax import lax

NEV = 2048
B = 64
PW = 256
SWEEPS = 8
NROWS = 106496
NWIN = 832


def draw_panel_t(key, part):
    key = jax.random.fold_in(key, 11)
    diag_key, off_key = jax.random.split(key)
    row_ids = lax.broadcasted_iota(jnp.int32, (2, PW, PW), 1)
    col_ids = lax.broadcasted_iota(jnp.int32, (2, PW, PW), 2)
    diag_part = jax.random.uniform(diag_key, (2, PW, PW), jnp.float32, 0.2, 1.8)
    off_part = jnp.clip(jax.random.normal(off_key, (2, PW, PW), jnp.float32), -3.0, 3.0) * (0.5 / PW ** 0.5)
    off_part = jnp.clip(off_part, -0.1, 0.1)
    return jnp.where(row_ids == col_ids, diag_part, jnp.where(row_ids < col_ids, off_part, 0.0)).astype(jnp.float32)


def level_of(own_key, extent, cuts, least, largest):
    def one(dim, blocks):
        heights = jax.random.uniform(jax.random.fold_in(jax.random.fold_in(own_key, 6), dim), (blocks,), jnp.float32, least / len(cuts), largest / len(cuts))
        return jnp.repeat(jnp.exp(heights), extent[dim] // blocks).reshape((-1,) + (1,) * (len(extent) - dim - 1))

    level = one(*cuts[0])
    for cut in cuts[1:]:
        level = level * one(*cut)
    return level


def centred(rng, extent, deviation, reach, cuts=(), held_as=jnp.bfloat16):
    factor_of = level_of(rng, extent, cuts, -0.22, 0.18) if cuts else 1.0
    entries = jax.random.normal(rng, extent, jnp.float32) * deviation * factor_of
    return jnp.minimum(jnp.maximum(entries, -reach), reach).astype(held_as)


def setup_inputs(seed: int = 0) -> dict:
    key_list = jax.random.split(jax.random.key(seed), 6)
    return {
        "eigvecs": centred(key_list[0], (NROWS, NEV), 1.0, 6.0, ((0, 32), (1, 8)), jnp.float32),
        "reflect_y": centred(key_list[1], (SWEEPS, NWIN, B, 2 * B), (2 * B) ** -0.5, 0.5, ((1, 32),), jnp.float32),
        "reflect_w": centred(key_list[2], (SWEEPS, NWIN, B, 2 * B), (16 * B) ** -0.5, 0.1875, ((1, 32),), jnp.float32),
        "panel_v": centred(key_list[3], (NROWS, 2 * PW), NROWS ** -0.5, 0.01953125, ((0, 32), (1, 8)), jnp.float32),
        "panel_t": draw_panel_t(jax.random.fold_in(key_list[5], 71), 0),
    }


def apply_windows(vectors, y_blocks, w_blocks):
    groups = y_blocks.shape[0]
    window_rows = vectors.reshape(groups, y_blocks.shape[2], vectors.shape[1])
    projected = jnp.einsum('wbk,wkc->wbc', y_blocks, window_rows, precision=lax.Precision.HIGHEST)
    window_rows = window_rows - jnp.einsum('wbk,wbc->wkc', w_blocks, projected, precision=lax.Precision.HIGHEST)
    return window_rows.reshape(vectors.shape)


def matmul(left, right):
    return jnp.dot(left, right, precision=lax.Precision.HIGHEST, preferred_element_type=jnp.float32)


def inner_product(left, right):
    return lax.dot_general(left, right, (((0,), (0,)), ((), ())), precision=lax.Precision.HIGHEST, preferred_element_type=jnp.float32)


def reference(eigvecs, reflect_y, reflect_w, panel_v, panel_t):
    vectors = eigvecs
    for sweep_index in range(SWEEPS):
        if sweep_index % 2 == 1:
            vectors = jnp.roll(vectors, -B, axis=0)
        vectors = apply_windows(vectors, reflect_y[sweep_index], reflect_w[sweep_index])
        if sweep_index % 2 == 1:
            vectors = jnp.roll(vectors, B, axis=0)
    for panel_index in range(2):
        panel = panel_v[:, panel_index * PW:(panel_index + 1) * PW]
        coeffs = inner_product(panel, vectors)
        vectors = vectors - matmul(panel, matmul(panel_t[panel_index], coeffs))
    return vectors
```

```python
import functools

import jax
import jax.numpy as jnp
from jax import lax
from jax.experimental import pallas as pl
from jax.experimental.pallas import tpu as pltpu
from jax.sharding import Mesh, PartitionSpec as P

HALO = 256
GROUP = 4
ANY = pl.BlockSpec(memory_space=pl.ANY)
F32 = jnp.float32
BF16 = jnp.bfloat16
VMEM_LIMIT = 48 * 1024 * 1024


def split(value):
    high = value.astype(BF16)
    low = (value - high.astype(F32)).astype(BF16)
    return high, low


def dot(left, right, dims=(((1,), (0,)), ((), ()))):
    return lax.dot_general(left, right, dims, preferred_element_type=F32)


def dot3(left, right, dims=(((1,), (0,)), ((), ()))):
    left_high, left_low = left
    right_high, right_low = right
    return (
        dot(left_high, right_low, dims) + dot(left_low, right_high, dims) + dot(left_high, right_high, dims)
    )


def band_steps(blocks):
    projected = []
    for z, y, _ in blocks:
        z_high, z_low = split(z)
        y_high, y_low = split(y)
        left = jnp.concatenate(
            [jnp.concatenate([y_high, y_high], axis=1), jnp.concatenate([y_low, y_low], axis=1)], axis=0
        )
        both = dot(left, jnp.concatenate([z_high, z_low], axis=0))
        half = y.shape[0]
        projected.append(both[:half] + both[half:])
    out = []
    for (z, _, w), p in zip(blocks, projected):
        p_high, p_low = split(p)
        w_high, w_low = split(w)
        turned = jnp.concatenate([w_high, w_low], axis=0).T
        left = jnp.concatenate([turned, turned], axis=1)
        out.append(z - dot(left, jnp.concatenate([p_high, p_high, p_low, p_low], axis=0)))
    return out


def interior_kernel(base, windows, x_ref, y_ref, w_ref, out_ref, x, y, w, x_sem, y_sem, w_sem):
    load = pltpu.make_async_copy(x_ref, x, x_sem)
    load.start()
    loads = []
    for s in range(4):
        pair = (
            pltpu.make_async_copy(y_ref.at[base + s], y.at[s], y_sem.at[s]),
            pltpu.make_async_copy(w_ref.at[base + s], w.at[s], w_sem.at[s]),
        )
        for copy in pair:
            copy.start()
        loads.append(pair)
    load.wait()
    for s in range(4):
        for copy in loads[s]:
            copy.wait()
        first = s // 2
        count = windows - s
        shift = 64 * (s % 2)

        def run(start, number, s=s, shift=shift):
            rows = [pl.ds(pl.multiple_of((start + j) * 128 + shift, 64), 128) for j in range(number)]
            blocks = [(x[rows[j], :], y[s, start + j], w[s, start + j]) for j in range(number)]
            for j, value in enumerate(band_steps(blocks)):
                x[rows[j], :] = value

        @pl.loop(0, count // GROUP)
        def _(i, first=first, run=run):
            run(first + i * GROUP, GROUP)

        rest = count % GROUP
        if rest:
            run(first + count - rest, rest)
    store = pltpu.make_async_copy(x, out_ref, x_sem)
    store.start()
    store.wait()


def interior(base, x, y, w):
    windows = y.shape[1]
    return pl.pallas_call(
        functools.partial(interior_kernel, base, windows),
        out_shape=jax.ShapeDtypeStruct(x.shape, F32),
        in_specs=[ANY] * 3,
        out_specs=ANY,
        scratch_shapes=[
            pltpu.VMEM(x.shape, F32),
            pltpu.VMEM((4,) + y.shape[1:], F32),
            pltpu.VMEM((4,) + w.shape[1:], F32),
            pltpu.SemaphoreType.DMA,
            pltpu.SemaphoreType.DMA((4,)),
            pltpu.SemaphoreType.DMA((4,)),
        ],
        compiler_params=pltpu.CompilerParams(vmem_limit_bytes=VMEM_LIMIT),
        cost_estimate=pl.CostEstimate(flops=10_000_000_000, bytes_accessed=14_000_000, transcendentals=0),
        name=f"interior{base}",
    )(x, y, w)


def boundary_plan(base, last):
    k = base // 4
    a, b = 6 * k, 4 * k
    return [
        [(0, 0, "above", a), (0, 128, "above", a + 1), (1, 256, "below", b), (1, 384, "below", b + 1)],
        [(0, 64, "above", a + 2), (0, 192, "above", a + 3), (1, 192, "own", (1, last)), (1, 320, "below", b + 2)],
        [(0, 128, "above", a + 4), (0, 256, "own", (2, 0)), (1, 128, "own", (2, last)), (1, 256, "below", b + 3)],
        [(0, 192, "above", a + 5), (0, 320, "own", (3, 0)), (1, 64, "own", (3, last - 1)), (1, 192, "own", (3, last))],
    ]


def boundary_kernel(base, last, with_edges, *refs):
    x_ref, halo_above, halo_below, y_ref, w_ref, above_ref, below_ref = refs[:7]
    out_ref = refs[7]
    edge_refs = refs[8:10] if with_edges else ()
    side, y, w, side_sem, refl_sem = refs[-5:]
    rows = x_ref.shape[0]
    copies = [
        pltpu.make_async_copy(halo_above, side.at[0, pl.ds(0, HALO)], side_sem.at[0]),
        pltpu.make_async_copy(x_ref.at[pl.ds(0, HALO)], side.at[0, pl.ds(HALO, HALO)], side_sem.at[1]),
        pltpu.make_async_copy(x_ref.at[pl.ds(rows - HALO, HALO)], side.at[1, pl.ds(0, HALO)], side_sem.at[2]),
        pltpu.make_async_copy(halo_below, side.at[1, pl.ds(HALO, HALO)], side_sem.at[3]),
    ]
    half_above = above_ref.shape[0] // 2
    half_below = below_ref.shape[0] // 2
    plan = boundary_plan(base, last)
    for s, steps in enumerate(plan):
        for j, (_, _, source, index) in enumerate(steps):
            slot = 4 * s + j
            if source == "above":
                y_source, w_source = above_ref.at[index], above_ref.at[half_above + index]
            elif source == "below":
                y_source, w_source = below_ref.at[index], below_ref.at[half_below + index]
            else:
                y_source = y_ref.at[base + index[0], index[1]]
                w_source = w_ref.at[base + index[0], index[1]]
            copies.append(pltpu.make_async_copy(y_source, y.at[slot], refl_sem.at[0, slot]))
            copies.append(pltpu.make_async_copy(w_source, w.at[slot], refl_sem.at[1, slot]))
    for copy in copies:
        copy.start()
    for copy in copies:
        copy.wait()
    for s, steps in enumerate(plan):
        blocks = [
            (side[which, pl.ds(row, 128), :], y[4 * s + j], w[4 * s + j])
            for j, (which, row, _, _) in enumerate(steps)
        ]
        for (which, row, _, _), value in zip(steps, band_steps(blocks)):
            side[which, pl.ds(row, 128), :] = value
    top, bottom = side.at[0, pl.ds(HALO, HALO)], side.at[1, pl.ds(0, HALO)]
    stores = [
        pltpu.make_async_copy(top, out_ref.at[pl.ds(0, HALO)], side_sem.at[0]),
        pltpu.make_async_copy(bottom, out_ref.at[pl.ds(rows - HALO, HALO)], side_sem.at[1]),
    ]
    if with_edges:
        stores.append(pltpu.make_async_copy(top, edge_refs[0], side_sem.at[2]))
        stores.append(pltpu.make_async_copy(bottom, edge_refs[1], side_sem.at[3]))
    for copy in stores:
        copy.start()
    for copy in stores:
        copy.wait()


def boundary(base, with_edges, x, halo_above, halo_below, y, w, above, below):
    edge = jax.ShapeDtypeStruct((HALO, x.shape[1]), F32)
    out_shape = [jax.ShapeDtypeStruct(x.shape, F32)] + [edge, edge] * with_edges
    return pl.pallas_call(
        functools.partial(boundary_kernel, base, y.shape[1] - 1, with_edges),
        out_shape=out_shape,
        in_specs=[ANY] * 7,
        out_specs=[ANY] * len(out_shape),
        scratch_shapes=[
            pltpu.VMEM((2, 2 * HALO, x.shape[1]), F32),
            pltpu.VMEM((16,) + y.shape[2:], F32),
            pltpu.VMEM((16,) + w.shape[2:], F32),
            pltpu.SemaphoreType.DMA((4,)),
            pltpu.SemaphoreType.DMA((2, 16)),
        ],
        input_output_aliases={0: 0},
        compiler_params=pltpu.CompilerParams(vmem_limit_bytes=VMEM_LIMIT),
        cost_estimate=pl.CostEstimate(flops=1_500_000_000, bytes_accessed=3_000_000, transcendentals=0),
        name=f"boundary{base}",
    )(x, halo_above, halo_below, y, w, above, below)


def place_pieces(places, pieces, panel):
    at = 0
    for number, piece in enumerate(pieces):
        height = piece.shape[0]
        panel[pl.ds(pl.multiple_of(places[number], 32), height), :] = piece[...]


def coeffs_kernel(shares, places, x_ref, *refs):
    pieces, out_ref, panel, coeffs, gram = refs[:-4], refs[-4], refs[-3], refs[-2], refs[-1]
    step = pl.program_id(0)
    place_pieces(places, pieces, panel)
    width = gram.shape[0]
    high, low = split(panel[...])
    part = dot3((high, low), split(x_ref[...]))
    gram_part = dot3(
        (high[width:], low[width:]), (high[:width], low[:width]), (((1,), (1,)), ((), ()))
    )

    @pl.when(step == 0)
    def _():
        coeffs[...] = part
        gram[...] = gram_part

    @pl.when(step > 0)
    def _():
        coeffs[...] += part
        gram[...] += gram_part

    @pl.when(step == pl.num_programs(0) - 1)
    def _():
        a, b = coeffs.shape[0] // shares, width // shares
        out_ref[:, :a, :] = coeffs[...].reshape(shares, a, -1)
        out_ref[:, a:, :] = gram[...].reshape(shares, b, -1)


def piece_specs(pieces, tile):
    return [pl.BlockSpec((piece.shape[0], tile), lambda i, _: (0, i)) for piece in pieces]


def panel_coeffs(shares, places, x, pieces, width):
    tile = 256
    rows, columns = x.shape
    out = jax.ShapeDtypeStruct((shares, 3 * width // shares, columns), F32)
    return pl.pallas_call(
        functools.partial(coeffs_kernel, shares),
        out_shape=out,
        grid_spec=pltpu.PrefetchScalarGridSpec(
            num_scalar_prefetch=1,
            grid=(rows // tile,),
            in_specs=[pl.BlockSpec((tile, columns), lambda i, _: (i, 0))] + piece_specs(pieces, tile),
            out_specs=pl.BlockSpec(out.shape, lambda i, _: (0, 0, 0)),
            scratch_shapes=[
                pltpu.VMEM((2 * width, tile), F32),
                pltpu.VMEM((2 * width, columns), F32),
                pltpu.VMEM((width, width), F32),
            ],
        ),
        compiler_params=pltpu.CompilerParams(vmem_limit_bytes=VMEM_LIMIT),
        cost_estimate=pl.CostEstimate(flops=4_000_000_000, bytes_accessed=11_000_000, transcendentals=0),
        name="panel_coeffs",
    )(places, x, *pieces)


def update_kernel(places, sums_ref, t_ref, x_ref, *refs):
    pieces, out_ref, panel, high, low = refs[:-4], refs[-4], refs[-3], refs[-2], refs[-1]
    width = t_ref.shape[1]

    @pl.when(pl.program_id(0) == 0)
    def _():
        shares = sums_ref.shape[0]
        a = 2 * width // shares
        coeffs = sums_ref[:, :a, :].reshape(2 * width, -1)
        gram = sums_ref[:, a:, :].reshape(width, width)
        first = dot3(split(t_ref[0]), split(coeffs[:width]))
        rest = coeffs[width:] - dot3(split(gram), split(first))
        second = dot3(split(t_ref[1]), split(rest))
        for start, value in ((0, first), (width, second)):
            value_high, value_low = split(value)
            high[start : start + width] = value_high
            low[start : start + width] = value_low

    place_pieces(places, pieces, panel)
    change = dot3(split(panel[...].T), (high[...], low[...]))
    out_ref[...] = x_ref[...] - change


def update(places, sums, t, x, pieces):
    tile = 256
    rows, columns = x.shape
    width = t.shape[1]
    whole = lambda shape: pl.BlockSpec(shape, lambda i, _: (0,) * len(shape))
    return pl.pallas_call(
        update_kernel,
        out_shape=jax.ShapeDtypeStruct(x.shape, F32),
        grid_spec=pltpu.PrefetchScalarGridSpec(
            num_scalar_prefetch=1,
            grid=(rows // tile,),
            in_specs=[whole(sums.shape), whole(t.shape), pl.BlockSpec((tile, columns), lambda i, _: (i, 0))]
            + piece_specs(pieces, tile),
            out_specs=pl.BlockSpec((tile, columns), lambda i, _: (i, 0)),
            scratch_shapes=[
                pltpu.VMEM((2 * width, tile), F32),
                pltpu.VMEM((2 * width, columns), BF16),
                pltpu.VMEM((2 * width, columns), BF16),
            ],
        ),
        compiler_params=pltpu.CompilerParams(vmem_limit_bytes=VMEM_LIMIT),
        cost_estimate=pl.CostEstimate(flops=3_000_000_000, bytes_accessed=14_000_000, transcendentals=0),
        name="update",
    )(places, sums, t, x, *pieces)


def send(value, axis, steps):
    count = lax.axis_size(axis)
    return lax.ppermute(value, axis, [(i, (i + steps) % count) for i in range(count)])


def per_device(eigvecs, reflect_y, reflect_w, panel_v, panel_t):
    rows = ("z", "y")
    shares = lax.axis_size(rows)
    last = reflect_y.shape[1] - 1
    width = panel_t.shape[1]
    own = panel_v.T
    height = own.shape[0]
    half = height // 2

    from_left = send(own, "x", 1)
    from_right = send(own, "x", -1)
    halo_above = send(eigvecs[-HALO:], rows, 1)
    halo_below = send(eigvecs[:HALO], rows, -1)

    def to_below(r):
        return [r[0:2, last - 1 :].reshape((4,) + r.shape[2:]), r[2:4, last], r[4:6, last - 1 :].reshape((4,) + r.shape[2:]), r[6:8, last]]

    def to_above(r):
        return [r[0, 0:2], r[1, 0:1], r[2, 0:1], r[4, 0:2], r[5, 0:1], r[6, 0:1]]

    above = send(jnp.concatenate(to_below(reflect_y) + to_below(reflect_w)), rows, 1)
    below = send(jnp.concatenate(to_above(reflect_y) + to_above(reflect_w)), rows, -1)
    twin_own = send(own, "core", 1)

    x = interior(0, eigvecs, reflect_y, reflect_w)
    x, top, bottom = boundary(0, True, x, halo_above, halo_below, reflect_y, reflect_w, above, below)
    halo_above = send(bottom, rows, 1)
    halo_below = send(top, rows, -1)

    across_low = send(from_left[:half], "x", 1)
    across_high = send(from_right[half:], "x", -1)
    twin_left = send(from_left, "core", 1)
    twin_right = send(from_right, "core", 1)

    x = interior(4, x, reflect_y, reflect_w)
    twin_across_low = send(across_low, "core", 1)
    twin_across_high = send(across_high, "core", 1)
    (x,) = boundary(4, False, x, halo_above, halo_below, reflect_y, reflect_w, above, below)

    pieces = [own, twin_own, from_left, twin_left, from_right, twin_right]
    pieces += [across_low, twin_across_low, across_high, twin_across_high]
    at_x, at_core = lax.axis_index("x"), lax.axis_index("core")
    places = []
    for shift, start in ((0, 0), (-1, 0), (1, 0), (2, 0), (2, half)):
        for twin in (0, 1):
            col = (at_x + shift) % 4 * 2 + (at_core + twin) % 2
            places.append(col * height + start)
    places = jnp.stack(places).astype(jnp.int32)

    sums = panel_coeffs(shares, places, x, pieces, width)
    mine = jnp.sum(lax.all_to_all(sums, rows, 0, 0), axis=0)
    sums = lax.all_to_all(jnp.broadcast_to(mine[None], sums.shape), rows, 0, 0)
    return update(places, sums, panel_t, x, pieces)


def solution(mesh):
    z, y, x, core = 8, 4, 4, 2
    fine = Mesh(mesh.devices.reshape(z, y, x, core), ("z", "y", "x", "core"))
    row, col = ("z", "y"), ("x", "core")
    return jax.shard_map(
        per_device,
        mesh=fine,
        in_specs=(
            P(row, col),
            P(None, row, None, None),
            P(None, row, None, None),
            P(row, col),
            P(),
        ),
        out_specs=P(row, col),
        check_vma=False,
    )
```

```python
import functools

import jax
import jax.numpy as jnp
from jax import lax
from jax.experimental import pallas as pl
from jax.experimental.pallas import tpu as pltpu
from jax.sharding import Mesh, PartitionSpec as P

HALO = 256
PARTS = 3
GROUP = 9
ANY = pl.BlockSpec(memory_space=pltpu.HBM)
F32 = jnp.float32
BF16 = jnp.bfloat16
VMEM_LIMIT = 65024 * 1024


def split(value):
    high = value.astype(BF16)
    low = (value - high.astype(F32)).astype(BF16)
    return high, low


def dot(left, right, dims=(((1,), (0,)), ((), ()))):
    return lax.dot_general(left, right, dims, preferred_element_type=F32)


def dot3(left, right, dims=(((1,), (0,)), ((), ()))):
    left_high, left_low = left
    right_high, right_low = right
    return (
        dot(left_high, right_low, dims) + dot(left_low, right_high, dims) + dot(left_high, right_high, dims)
    )


def band_steps(blocks):
    projected = []
    for z, y, _ in blocks:
        z_high, z_low = split(z)
        y_high, y_low = split(y)
        left = jnp.concatenate(
            [jnp.concatenate([y_high, y_high], axis=1), jnp.concatenate([y_low, y_low], axis=1)], axis=0
        )
        both = dot(left, jnp.concatenate([z_high, z_low], axis=0))
        half = y.shape[0]
        projected.append(both[:half] + both[half:])
    out = []
    for (z, _, w), p in zip(blocks, projected):
        p_high, p_low = split(p)
        w_high, w_low = split(w)
        turned = jnp.concatenate([w_high, w_low], axis=0).T
        left = jnp.concatenate([turned, turned], axis=1)
        out.append(z - dot(left, jnp.concatenate([p_high, p_high, p_low, p_low], axis=0)))
    return out


def interior_kernel(base, x_ref, y_ref, w_ref, out_ref, x, y, w, first_sem, sweep_sem, store_sem):
    rows, windows = x.shape[0], y.shape[1]
    cuts = [windows * part // PARTS for part in range(PARTS + 1)]
    first, later = [], []
    for part in range(PARTS):
        start, number = cuts[part], cuts[part + 1] - cuts[part]
        span = pl.ds(start * 128, number * 128)
        some = pl.ds(start, number)
        first.append(
            (
                pltpu.make_async_copy(x_ref.at[span], x.at[span], first_sem.at[0, part]),
                pltpu.make_async_copy(y_ref.at[base, some], y.at[0, some], first_sem.at[1, part]),
                pltpu.make_async_copy(w_ref.at[base, some], w.at[0, some], first_sem.at[2, part]),
            )
        )
    for s in range(1, 4):
        later.append(
            (
                pltpu.make_async_copy(y_ref.at[base + s], y.at[s], sweep_sem.at[0, s]),
                pltpu.make_async_copy(w_ref.at[base + s], w.at[s], sweep_sem.at[1, s]),
            )
        )
    for copies in first + later:
        for copy in copies:
            copy.start()

    def run(s, start, stop):
        rows_of = [pl.ds(v * 128 + 64 * (s % 2), 128) for v in range(start, stop)]
        blocks = [(x[at, :], y[s, v], w[s, v]) for at, v in zip(rows_of, range(start, stop))]
        for at, value in zip(rows_of, band_steps(blocks)):
            x[at, :] = value

    for part in range(PARTS):
        for copy in first[part]:
            copy.wait()
        run(0, cuts[part], cuts[part + 1])
    stores = []
    stored = 0
    for s in range(1, 4):
        for copy in later[s - 1]:
            copy.wait()
        begin, end = s // 2, s // 2 + windows - s
        for start in range(begin, end, GROUP):
            stop = min(start + GROUP, end)
            run(s, start, stop)
            if s == 3:
                until = rows if stop == end else stop * 128 + 64
                span = pl.ds(stored, until - stored)
                stores.append(pltpu.make_async_copy(x.at[span], out_ref.at[span], store_sem.at[len(stores)]))
                stores[-1].start()
                stored = until
    for copy in stores:
        copy.wait()


def interior(base, x, y, w):
    return pl.pallas_call(
        functools.partial(interior_kernel, base),
        out_shape=jax.ShapeDtypeStruct(x.shape, F32),
        in_specs=[ANY] * 3,
        out_specs=ANY,
        scratch_shapes=[
            pltpu.VMEM(x.shape, F32),
            pltpu.VMEM((4,) + y.shape[1:], F32),
            pltpu.VMEM((4,) + w.shape[1:], F32),
            pltpu.SemaphoreType.DMA((3, PARTS)),
            pltpu.SemaphoreType.DMA((2, 4)),
            pltpu.SemaphoreType.DMA((8,)),
        ],
        compiler_params=pltpu.CompilerParams(vmem_limit_bytes=VMEM_LIMIT),
        cost_estimate=pl.CostEstimate(flops=10_000_000_000, bytes_accessed=14_000_000, transcendentals=0),
        name=f"interior{base}",
    )(x, y, w)


def to_below(last):
    return [(0, last - 1, 2), (1, last - 1, 2), (2, last, 1), (3, last, 1)]


def to_above(last):
    return [(0, 0, 2), (1, 0, 1), (2, 0, 1)]


def bundle_rows(plan):
    return 2 * HALO + 2 * 64 * sum(number for _, _, number in plan)


def bundle_copies(edge, y_ref, w_ref, base, plan, out, sem):
    copies = []

    def copy(source, at, rows):
        copies.append(pltpu.make_async_copy(source, out.at[pl.ds(at, rows)], sem.at[len(copies)]))
        return at + rows

    at = 0
    for lane in (0, 128):
        at = copy(edge.at[:, pl.ds(lane, 128)], at, HALO)
    for source in (y_ref, w_ref):
        for sweep, start, number in plan:
            for j in range(number):
                at = copy(source.at[base + sweep, start + j], at, 64)
    return copies


def pack_kernel(rows, last, x_ref, y_ref, w_ref, below_ref, above_ref, sem):
    bottom, top = x_ref.at[pl.ds(rows - HALO, HALO)], x_ref.at[pl.ds(0, HALO)]
    copies = bundle_copies(bottom, y_ref, w_ref, 0, to_below(last), below_ref, sem.at[0])
    copies += bundle_copies(top, y_ref, w_ref, 0, to_above(last), above_ref, sem.at[1])
    for copy in copies:
        copy.start()
    for copy in copies:
        copy.wait()


def bundles(last):
    return [jax.ShapeDtypeStruct((bundle_rows(plan), 128), F32) for plan in (to_below(last), to_above(last))]


def pack(x, y, w):
    rows, last = x.shape[0], y.shape[1] - 1
    return pl.pallas_call(
        functools.partial(pack_kernel, rows, last),
        out_shape=bundles(last),
        in_specs=[ANY] * 3,
        out_specs=[ANY] * 2,
        scratch_shapes=[pltpu.SemaphoreType.DMA((2, 16))],
        compiler_params=pltpu.CompilerParams(vmem_limit_bytes=VMEM_LIMIT),
        cost_estimate=pl.CostEstimate(flops=0, bytes_accessed=4_000_000, transcendentals=0),
        name="pack",
    )(x, y, w)


def boundary_plan(last):
    return [
        [(0, 0, "above", 0), (0, 128, "above", 1), (1, 256, "below", 0), (1, 384, "below", 1)],
        [(0, 64, "above", 2), (0, 192, "above", 3), (1, 192, "own", (1, last)), (1, 320, "below", 2)],
        [(0, 128, "above", 4), (0, 256, "own", (2, 0)), (1, 128, "own", (2, last)), (1, 256, "below", 3)],
        [(0, 192, "above", 5), (0, 320, "own", (3, 0)), (1, 64, "own", (3, last - 1)), (1, 192, "own", (3, last))],
    ]


def boundary_kernel(base, last, hand, *refs):
    x_ref, y_ref, w_ref, above_ref, below_ref = refs[:5]
    side, y, w, side_sem, refl_sem, pass_sem, send_sem = refs[-7:]
    rows = x_ref.shape[0]
    passing = []
    if hand:
        left_ref, right_ref, _, out_ref, to_below_ref, to_above_ref, duo_ref, low_ref, high_ref = refs[5:-7]
        height = left_ref.shape[0]
        half = height // 2
        passing = [
            pltpu.make_async_copy(left_ref.at[pl.ds(0, half)], low_ref, pass_sem.at[0]),
            pltpu.make_async_copy(right_ref.at[pl.ds(half, half)], high_ref, pass_sem.at[1]),
            pltpu.make_async_copy(left_ref, duo_ref.at[pl.ds(0, height)], pass_sem.at[2]),
            pltpu.make_async_copy(right_ref, duo_ref.at[pl.ds(height, height)], pass_sem.at[3]),
        ]
    else:
        (out_ref,) = refs[5:-7]
    loads = [
        pltpu.make_async_copy(x_ref.at[pl.ds(0, HALO)], side.at[0, pl.ds(HALO, HALO)], side_sem.at[0]),
        pltpu.make_async_copy(x_ref.at[pl.ds(rows - HALO, HALO)], side.at[1, pl.ds(0, HALO)], side_sem.at[1]),
    ]
    for j in range(2):
        rows_j, lanes = pl.ds(j * HALO, HALO), pl.ds(j * 128, 128)
        loads.append(
            pltpu.make_async_copy(above_ref.at[rows_j], side.at[0, pl.ds(0, HALO), lanes], side_sem.at[2 + j])
        )
        loads.append(
            pltpu.make_async_copy(below_ref.at[rows_j], side.at[1, pl.ds(HALO, HALO), lanes], side_sem.at[4 + j])
        )
    half_above = (above_ref.shape[0] - 2 * HALO) // 2
    half_below = (below_ref.shape[0] - 2 * HALO) // 2
    plan = boundary_plan(last)
    waits = []
    for s, steps in enumerate(plan):
        sweep = []
        for j, (_, _, source, index) in enumerate(steps):
            slot = 4 * s + j
            if source == "own":
                y_source = y_ref.at[base + index[0], index[1]]
                w_source = w_ref.at[base + index[0], index[1]]
            else:
                ref, skip = (above_ref, half_above) if source == "above" else (below_ref, half_below)
                y_source = ref.at[pl.ds(2 * HALO + 64 * index, 64)]
                w_source = ref.at[pl.ds(2 * HALO + skip + 64 * index, 64)]
            sweep.append(pltpu.make_async_copy(y_source, y.at[slot], refl_sem.at[0, slot]))
            sweep.append(pltpu.make_async_copy(w_source, w.at[slot], refl_sem.at[1, slot]))
        waits.append(sweep)
    for copies in [loads] + waits + [passing]:
        for copy in copies:
            copy.start()
    for copy in loads:
        copy.wait()
    for s, steps in enumerate(plan):
        for copy in waits[s]:
            copy.wait()
        blocks = [
            (side[which, pl.ds(row, 128), :], y[4 * s + j], w[4 * s + j])
            for j, (which, row, _, _) in enumerate(steps)
        ]
        for (which, row, _, _), value in zip(steps, band_steps(blocks)):
            side[which, pl.ds(row, 128), :] = value
    top, bottom = side.at[0, pl.ds(HALO, HALO)], side.at[1, pl.ds(0, HALO)]
    stores = [
        pltpu.make_async_copy(top, out_ref.at[pl.ds(0, HALO)], side_sem.at[0]),
        pltpu.make_async_copy(bottom, out_ref.at[pl.ds(rows - HALO, HALO)], side_sem.at[1]),
    ]
    if hand:
        stores += bundle_copies(bottom, y_ref, w_ref, base + 4, to_below(last), to_below_ref, send_sem.at[0])
        stores += bundle_copies(top, y_ref, w_ref, base + 4, to_above(last), to_above_ref, send_sem.at[1])
    for copy in stores:
        copy.start()
    for copy in stores + passing:
        copy.wait()


def boundary(base, x, y, w, above, below, beside=()):
    last = y.shape[1] - 1
    out_shape = [jax.ShapeDtypeStruct(x.shape, F32)]
    if beside:
        height, rows = beside[0].shape
        out_shape += bundles(last) + [
            jax.ShapeDtypeStruct((part, rows), F32) for part in (2 * height, height // 2, height // 2)
        ]
    return pl.pallas_call(
        functools.partial(boundary_kernel, base, last, bool(beside)),
        out_shape=out_shape,
        in_specs=[ANY] * (5 + len(beside)),
        out_specs=[ANY] * len(out_shape),
        scratch_shapes=[
            pltpu.VMEM((2, 2 * HALO, x.shape[1]), F32),
            pltpu.VMEM((16,) + y.shape[2:], F32),
            pltpu.VMEM((16,) + w.shape[2:], F32),
            pltpu.SemaphoreType.DMA((6,)),
            pltpu.SemaphoreType.DMA((2, 16)),
            pltpu.SemaphoreType.DMA((4,)),
            pltpu.SemaphoreType.DMA((2, 16)),
        ],
        input_output_aliases={0: 0},
        compiler_params=pltpu.CompilerParams(vmem_limit_bytes=VMEM_LIMIT),
        cost_estimate=pl.CostEstimate(flops=1_500_000_000, bytes_accessed=3_000_000, transcendentals=0),
        name=f"boundary{base}",
    )(x, y, w, above, below, *beside)


def join_kernel(x_ref, low_ref, high_ref, above_ref, below_ref, out_ref, across_ref, sem):
    half = low_ref.shape[0]
    copies = [
        pltpu.make_async_copy(low_ref, across_ref.at[pl.ds(0, half)], sem.at[0]),
        pltpu.make_async_copy(high_ref, across_ref.at[pl.ds(half, half)], sem.at[1]),
    ]
    for copy in copies:
        copy.start()
    for copy in copies:
        copy.wait()


def join(x, low, high, *beside):
    return pl.pallas_call(
        join_kernel,
        out_shape=[
            jax.ShapeDtypeStruct(x.shape, F32),
            jax.ShapeDtypeStruct((2 * low.shape[0], low.shape[1]), F32),
        ],
        in_specs=[ANY] * 5,
        out_specs=[ANY] * 2,
        scratch_shapes=[pltpu.SemaphoreType.DMA((2,))],
        input_output_aliases={0: 0},
        compiler_params=pltpu.CompilerParams(vmem_limit_bytes=VMEM_LIMIT),
        cost_estimate=pl.CostEstimate(flops=0, bytes_accessed=2_000_000, transcendentals=0),
        name="join",
    )(x, low, high, *beside)


SPANS = ((0, 1536), (1536, 1792))
TILE = 256
BY_ROWS = (((1,), (1,)), ((), ()))


def panel_loads(places, x_ref, pieces, x, panel, x_sem, sem):
    loads = []
    for number, (start, length) in enumerate(SPANS):
        span = pl.ds(start, length)
        copies = [pltpu.make_async_copy(x_ref.at[span], x.at[span], x_sem.at[number])]
        height = pieces[0].shape[0]
        slot = 0
        for piece in pieces:
            for at in range(0, piece.shape[0], height):
                rows = pl.ds(pl.multiple_of(places[slot], height), height)
                copies.append(
                    pltpu.make_async_copy(piece.at[pl.ds(at, height), span], panel.at[rows, span], sem.at[number, slot])
                )
                slot += 1
        loads.append(copies)
    for copies in loads:
        for copy in copies:
            copy.start()
    return loads


def coeffs_kernel(shares, width, places, x_ref, *refs):
    *pieces, out_ref, panel, x, x_sem, sem = refs
    loads = panel_loads(places, x_ref, pieces, x, panel, x_sem, sem)
    coeffs = gram = None
    for (start, length), copies in zip(SPANS, loads):
        for copy in copies:
            copy.wait()
        span = slice(start, start + length)
        high, low = split(panel[:, span])
        x_high, x_low = split(x[span, :])
        part = dot(
            jnp.concatenate([high, low, high], axis=1), jnp.concatenate([x_high, x_high, x_low], axis=0)
        )
        gram_part = dot(
            jnp.concatenate([high[width:], low[width:], high[width:]], axis=1),
            jnp.concatenate([high[:width], high[:width], low[:width]], axis=1),
            BY_ROWS,
        )
        coeffs = part if coeffs is None else coeffs + part
        gram = gram_part if gram is None else gram + gram_part
    a, b = 2 * width // shares, width // shares
    out_ref[:, :a, :] = coeffs.reshape(shares, a, -1)
    out_ref[:, a:, :] = gram.reshape(shares, b, -1)


SMEM_SPEC = pl.BlockSpec(memory_space=pltpu.SMEM)
VMEM_SPEC = pl.BlockSpec(memory_space=pltpu.VMEM)


def panel_coeffs(shares, places, x, pieces, width):
    rows, columns = x.shape
    return pl.pallas_call(
        functools.partial(coeffs_kernel, shares, width),
        out_shape=jax.ShapeDtypeStruct((shares, 3 * width // shares, columns), F32),
        in_specs=[SMEM_SPEC] + [ANY] * (1 + len(pieces)),
        out_specs=VMEM_SPEC,
        scratch_shapes=[
            pltpu.VMEM((2 * width, rows), F32),
            pltpu.VMEM(x.shape, F32),
            pltpu.SemaphoreType.DMA((2,)),
            pltpu.SemaphoreType.DMA((2, 8)),
        ],
        compiler_params=pltpu.CompilerParams(vmem_limit_bytes=VMEM_LIMIT),
        cost_estimate=pl.CostEstimate(flops=4_000_000_000, bytes_accessed=11_000_000, transcendentals=0),
        name="panel_coeffs",
    )(places, x, *pieces)


def update_kernel(places, sums_ref, t_ref, x_ref, *refs):
    *pieces, out_ref, panel, x, x_sem, sem, store_sem = refs
    loads = panel_loads(places, x_ref, pieces, x, panel, x_sem, sem)
    width = t_ref.shape[1]
    shares = sums_ref.shape[0]
    a = 2 * width // shares
    coeffs = sums_ref[:, :a, :].reshape(2 * width, -1)
    gram = sums_ref[:, a:, :].reshape(width, width)
    first = dot3(split(t_ref[0]), split(coeffs[:width]))
    rest = coeffs[width:] - dot3(split(gram), split(first))
    second = dot3(split(t_ref[1]), split(rest))
    high, low = split(jnp.concatenate([first, second], axis=0))
    right = jnp.concatenate([high, high, low], axis=0)
    stores = []
    for number, ((start, length), copies) in enumerate(zip(SPANS, loads)):
        for copy in copies:
            copy.wait()
        for at in range(start, start + length, TILE):
            span = slice(at, at + TILE)
            high, low = split(panel[:, span])
            high, low = high.T, low.T
            x[span, :] = x[span, :] - dot(jnp.concatenate([high, low, high], axis=1), right)
        span = pl.ds(start, length)
        stores.append(pltpu.make_async_copy(x.at[span], out_ref.at[span], store_sem.at[number]))
        stores[-1].start()
    for copy in stores:
        copy.wait()


def update(places, sums, t, x, pieces):
    rows = x.shape[0]
    return pl.pallas_call(
        update_kernel,
        out_shape=jax.ShapeDtypeStruct(x.shape, F32),
        in_specs=[SMEM_SPEC, VMEM_SPEC, VMEM_SPEC] + [ANY] * (1 + len(pieces)),
        out_specs=ANY,
        scratch_shapes=[
            pltpu.VMEM((2 * t.shape[1], rows), F32),
            pltpu.VMEM(x.shape, F32),
            pltpu.SemaphoreType.DMA((2,)),
            pltpu.SemaphoreType.DMA((2, 8)),
            pltpu.SemaphoreType.DMA((2,)),
        ],
        compiler_params=pltpu.CompilerParams(vmem_limit_bytes=VMEM_LIMIT),
        cost_estimate=pl.CostEstimate(flops=3_000_000_000, bytes_accessed=14_000_000, transcendentals=0),
        name="update",
    )(places, sums, t, x, *pieces)


def send(value, axis, steps):
    count = lax.axis_size(axis)
    return lax.ppermute(value, axis, [(i, (i + steps) % count) for i in range(count)])


def per_device(eigvecs, reflect_y, reflect_w, panel_v, panel_t):
    rows = ("z", "y")
    shares = lax.axis_size(rows)
    width = panel_t.shape[1]
    own = panel_v.T
    height = own.shape[0]

    from_left = send(own, "x", 1)
    from_right = send(own, "x", -1)
    for_below, for_above = pack(eigvecs, reflect_y, reflect_w)
    above, below = send(for_below, rows, 1), send(for_above, rows, -1)
    twin_own = send(own, "core", 1)

    x = interior(0, eigvecs, reflect_y, reflect_w)
    x, for_below, for_above, duo, low, high = boundary(
        0, x, reflect_y, reflect_w, above, below, (from_left, from_right, twin_own)
    )
    above, below = send(for_below, rows, 1), send(for_above, rows, -1)
    low = send(low, "x", 1)
    high = send(high, "x", -1)
    twin_duo = send(duo, "core", 1)

    x = interior(4, x, reflect_y, reflect_w)
    x, across = join(x, low, high, above, below)
    twin_across = send(across, "core", 1)
    (x,) = boundary(4, x, reflect_y, reflect_w, above, below)

    pieces = [own, twin_own, duo, twin_duo, across, twin_across]
    at_x, at_core = lax.axis_index("x"), lax.axis_index("core")
    places = []
    for shifts in ((0,), (-1, 1), (2,)):
        for twin in (0, 1):
            for shift in shifts:
                col = (at_x + shift) % 4 * 2 + (at_core + twin) % 2
                places.append(col * height)
    places = jnp.stack(places).astype(jnp.int32)

    sums = panel_coeffs(shares, places, x, pieces, width)
    mine = jnp.sum(lax.all_to_all(sums, rows, 0, 0), axis=0)
    sums = lax.all_to_all(jnp.broadcast_to(mine[None], sums.shape), rows, 0, 0)
    return update(places, sums, panel_t, x, pieces)


def solution(mesh):
    z, y, x, core = 8, 4, 4, 2
    fine = Mesh(mesh.devices.reshape(z, y, x, core), ("z", "y", "x", "core"))
    row, col = ("z", "y"), ("x", "core")
    return jax.shard_map(
        per_device,
        mesh=fine,
        in_specs=(
            P(row, col),
            P(None, row, None, None),
            P(None, row, None, None),
            P(row, col),
            P(),
        ),
        out_specs=P(row, col),
        check_vma=False,
    )
```

```python
import functools

import jax
import jax.numpy as jnp
from jax import lax
from jax.experimental import pallas as pl
from jax.experimental.pallas import tpu as pltpu
from jax.sharding import Mesh, PartitionSpec as P

HALO = 128
EDGE = 256
PARTS = 3
GROUP = 9
ANY = pl.BlockSpec(memory_space=pltpu.HBM)
F32 = jnp.float32
BF16 = jnp.bfloat16
VMEM_LIMIT = 65024 * 1024


def split(value):
    high = value.astype(BF16)
    low = (value - high.astype(F32)).astype(BF16)
    return high, low


def dot(left, right, dims=(((1,), (0,)), ((), ()))):
    return lax.dot_general(left, right, dims, preferred_element_type=F32)


def dot3(left, right, dims=(((1,), (0,)), ((), ()))):
    left_high, left_low = left
    right_high, right_low = right
    return (
        dot(left_high, right_low, dims) + dot(left_low, right_high, dims) + dot(left_high, right_high, dims)
    )


def band_steps(blocks):
    projected = []
    for z, y, _ in blocks:
        z_high, z_low = split(z)
        y_high, y_low = split(y)
        left = jnp.concatenate(
            [jnp.concatenate([y_high, y_high], axis=1), jnp.concatenate([y_low, y_low], axis=1)], axis=0
        )
        both = dot(left, jnp.concatenate([z_high, z_low], axis=0))
        half = y.shape[0]
        projected.append(both[:half] + both[half:])
    out = []
    for (z, _, w), p in zip(blocks, projected):
        p_high, p_low = split(p)
        w_high, w_low = split(w)
        turned = jnp.concatenate([w_high, w_low], axis=0).T
        left = jnp.concatenate([turned, turned], axis=1)
        out.append(z - dot(left, jnp.concatenate([p_high, p_high, p_low, p_low], axis=0)))
    return out


def interior_kernel(base, x_ref, y_ref, w_ref, out_ref, x, y, w, first_sem, sweep_sem, store_sem):
    rows, windows = x.shape[0], y.shape[1]
    cuts = [windows * part // PARTS for part in range(PARTS + 1)]
    first, later = [], []
    for part in range(PARTS):
        start, number = cuts[part], cuts[part + 1] - cuts[part]
        span = pl.ds(start * 128, number * 128)
        some = pl.ds(start, number)
        first.append(
            (
                pltpu.make_async_copy(x_ref.at[span], x.at[span], first_sem.at[0, part]),
                pltpu.make_async_copy(y_ref.at[base, some], y.at[0, some], first_sem.at[1, part]),
                pltpu.make_async_copy(w_ref.at[base, some], w.at[0, some], first_sem.at[2, part]),
            )
        )
    for s in range(1, 4):
        later.append(
            (
                pltpu.make_async_copy(y_ref.at[base + s], y.at[s], sweep_sem.at[0, s]),
                pltpu.make_async_copy(w_ref.at[base + s], w.at[s], sweep_sem.at[1, s]),
            )
        )
    for copies in first + later:
        for copy in copies:
            copy.start()

    def run(s, start, stop):
        rows_of = [pl.ds(v * 128 + 64 * (s % 2), 128) for v in range(start, stop)]
        blocks = [(x[at, :], y[s, v], w[s, v]) for at, v in zip(rows_of, range(start, stop))]
        for at, value in zip(rows_of, band_steps(blocks)):
            x[at, :] = value

    for part in range(PARTS):
        for copy in first[part]:
            copy.wait()
        run(0, cuts[part], cuts[part + 1])
    stores = []
    stored = 0
    for s in range(1, 4):
        for copy in later[s - 1]:
            copy.wait()
        begin, end = s // 2, s // 2 + windows - s
        for start in range(begin, end, GROUP):
            stop = min(start + GROUP, end)
            run(s, start, stop)
            if s == 3:
                until = rows if stop == end else stop * 128 + 64
                span = pl.ds(stored, until - stored)
                stores.append(pltpu.make_async_copy(x.at[span], out_ref.at[span], store_sem.at[len(stores)]))
                stores[-1].start()
                stored = until
    for copy in stores:
        copy.wait()


def interior(base, x, y, w):
    return pl.pallas_call(
        functools.partial(interior_kernel, base),
        out_shape=jax.ShapeDtypeStruct(x.shape, F32),
        in_specs=[ANY] * 3,
        out_specs=ANY,
        scratch_shapes=[
            pltpu.VMEM(x.shape, F32),
            pltpu.VMEM((4,) + y.shape[1:], F32),
            pltpu.VMEM((4,) + w.shape[1:], F32),
            pltpu.SemaphoreType.DMA((3, PARTS)),
            pltpu.SemaphoreType.DMA((2, 4)),
            pltpu.SemaphoreType.DMA((8,)),
        ],
        compiler_params=pltpu.CompilerParams(vmem_limit_bytes=VMEM_LIMIT),
        cost_estimate=pl.CostEstimate(flops=10_000_000_000, bytes_accessed=14_000_000, transcendentals=0),
        name=f"interior{base}",
    )(x, y, w)


def prepare_plan(base, last):
    return [
        [
            (0, 128, "own", (base, 0)),
            (0, 256, "own", (base, 1)),
            (1, 0, "own", (base, last - 1)),
            (1, 128, "own", (base, last)),
        ],
        [(0, 192, "own", (base + 1, 0)), (1, 64, "own", (base + 1, last - 1))],
    ]


def finish_plan(base, last):
    return [
        [(0, 64, "above", 0), (1, 192, "own", (base + 1, last))],
        [
            (0, 0, "above", 1),
            (0, 128, "own", (base + 2, 0)),
            (1, 128, "own", (base + 2, last)),
            (1, 256, "below", 0),
        ],
        [
            (0, 64, "above", 2),
            (0, 192, "own", (base + 3, 0)),
            (1, 64, "own", (base + 3, last - 1)),
            (1, 192, "own", (base + 3, last)),
        ],
    ]


def sent_reflectors(base, last):
    return [(base + 1, last), (base + 2, last), (base + 3, last)], [(base + 2, 0)]


def bundles(last):
    return [
        jax.ShapeDtypeStruct((2 * HALO + 2 * 64 * len(windows), 128), F32) for windows in sent_reflectors(0, last)
    ]


def edge_kernel(finish, prepare, last, *refs):
    refs = list(refs)
    take = lambda number: [refs.pop(0) for _ in range(number)]
    x_ref, y_ref, w_ref = take(3)
    above_ref = below_ref = None
    if finish is not None:
        above_ref, below_ref = take(2)
    both = finish is not None and prepare is not None
    if both:
        left_ref, right_ref, _ = take(3)
    if finish is not None:
        (out_ref,) = take(1)
    if prepare is not None:
        bundle_refs = take(2)
    if both:
        duo_ref, low_ref, high_ref = take(3)
    side, y, w, duo, sem = refs
    rows = x_ref.shape[0]
    used = [0]

    def copy(source, target):
        used[0] += 1
        return pltpu.make_async_copy(source, target, sem.at[used[0] - 1])

    def start(copies):
        for one in copies:
            one.start()

    def wait(copies):
        for one in copies:
            one.wait()

    loads = [
        copy(x_ref.at[pl.ds(0, EDGE)], side.at[0, pl.ds(HALO, EDGE)]),
        copy(x_ref.at[pl.ds(rows - EDGE, EDGE)], side.at[1, pl.ds(0, EDGE)]),
    ]
    if finish is not None:
        for j in range(2):
            part, lanes = pl.ds(j * HALO, HALO), pl.ds(j * 128, 128)
            loads.append(copy(above_ref.at[part], side.at[0, pl.ds(0, HALO), lanes]))
            loads.append(copy(below_ref.at[part], side.at[1, pl.ds(EDGE, HALO), lanes]))
    start(loads)

    stages = []
    if finish is not None:
        stages += finish_plan(finish, last)
    if prepare is not None:
        stages += prepare_plan(prepare, last)
    slot = 0
    slots, waits = [], []
    for steps in stages:
        mine, copies = [], []
        for _, _, source, index in steps:
            if source == "own":
                y_source, w_source = y_ref.at[index], w_ref.at[index]
            else:
                ref = above_ref if source == "above" else below_ref
                height = (ref.shape[0] - 2 * HALO) // 2
                y_source = ref.at[pl.ds(2 * HALO + 64 * index, 64)]
                w_source = ref.at[pl.ds(2 * HALO + height + 64 * index, 64)]
            copies += [copy(y_source, y.at[slot]), copy(w_source, w.at[slot])]
            mine.append(slot)
            slot += 1
        start(copies)
        slots.append(mine)
        waits.append(copies)
    passing, sending = [], []
    if prepare is not None:
        for windows, out in zip(sent_reflectors(prepare, last), bundle_refs):
            at = 2 * HALO
            for index in windows:
                passing += [copy(y_ref.at[index], y.at[slot]), copy(w_ref.at[index], w.at[slot])]
                sending += [
                    copy(y.at[slot], out.at[pl.ds(at, 64)]),
                    copy(w.at[slot], out.at[pl.ds(at + 64 * len(windows), 64)]),
                ]
                slot += 1
                at += 64
    if both:
        height = left_ref.shape[0]
        half = height // 2
        passing += [copy(left_ref, duo.at[pl.ds(0, height)]), copy(right_ref, duo.at[pl.ds(height, height)])]
        sending += [
            copy(duo, duo_ref),
            copy(duo.at[pl.ds(0, half)], low_ref),
            copy(duo.at[pl.ds(height + half, half)], high_ref),
        ]
    start(passing)
    wait(loads)

    def stage(number):
        wait(waits[number])
        blocks = [
            (side[which, pl.ds(row, 128), :], y[slots[number][j]], w[slots[number][j]])
            for j, (which, row, _, _) in enumerate(stages[number])
        ]
        for (which, row, _, _), value in zip(stages[number], band_steps(blocks)):
            side[which, pl.ds(row, 128), :] = value

    stores = []
    first = 0
    if finish is not None:
        first = 3
        for number in range(first):
            stage(number)
        stores = [
            copy(side.at[0, pl.ds(HALO, EDGE)], out_ref.at[pl.ds(0, EDGE)]),
            copy(side.at[1, pl.ds(0, EDGE)], out_ref.at[pl.ds(rows - EDGE, EDGE)]),
        ]
        start(stores)
    wait(passing)
    start(sending)
    if prepare is not None:
        wait(stores)
        stores = []
        for number in range(first, first + 2):
            stage(number)
        for j in range(2):
            part, lanes = pl.ds(j * HALO, HALO), pl.ds(j * 128, 128)
            stores.append(copy(side.at[1, pl.ds(EDGE - HALO, HALO), lanes], bundle_refs[0].at[part]))
            stores.append(copy(side.at[0, pl.ds(HALO, HALO), lanes], bundle_refs[1].at[part]))
        start(stores)
    wait(stores + sending)


def edges(finish, prepare, x, y, w, halos=(), beside=()):
    last = y.shape[1] - 1
    out_shape = []
    if finish is not None:
        out_shape.append(jax.ShapeDtypeStruct(x.shape, F32))
    if prepare is not None:
        out_shape += bundles(last)
    duo = (8, 128)
    if beside:
        height, rows = beside[0].shape
        duo = (2 * height, rows)
        out_shape += [jax.ShapeDtypeStruct((part, rows), F32) for part in (2 * height, height // 2, height // 2)]
    return pl.pallas_call(
        functools.partial(edge_kernel, finish, prepare, last),
        out_shape=out_shape,
        in_specs=[ANY] * (3 + len(halos) + len(beside)),
        out_specs=[ANY] * len(out_shape),
        scratch_shapes=[
            pltpu.VMEM((2, HALO + EDGE, x.shape[1]), F32),
            pltpu.VMEM((20,) + y.shape[2:], F32),
            pltpu.VMEM((20,) + w.shape[2:], F32),
            pltpu.VMEM(duo, F32),
            pltpu.SemaphoreType.DMA((80,)),
        ],
        input_output_aliases={} if finish is None else {0: 0},
        compiler_params=pltpu.CompilerParams(vmem_limit_bytes=VMEM_LIMIT),
        cost_estimate=pl.CostEstimate(flops=1_500_000_000, bytes_accessed=3_000_000, transcendentals=0),
        name="edges",
    )(x, y, w, *halos, *beside)


def join_kernel(x_ref, low_ref, high_ref, above_ref, below_ref, out_ref, across_ref, across, sem):
    half = low_ref.shape[0]
    loads = [
        pltpu.make_async_copy(low_ref, across.at[pl.ds(0, half)], sem.at[0]),
        pltpu.make_async_copy(high_ref, across.at[pl.ds(half, half)], sem.at[1]),
    ]
    for copy in loads:
        copy.start()
    for copy in loads:
        copy.wait()
    store = pltpu.make_async_copy(across, across_ref, sem.at[0])
    store.start()
    store.wait()


def join(x, low, high, *beside):
    across = (2 * low.shape[0], low.shape[1])
    return pl.pallas_call(
        join_kernel,
        out_shape=[jax.ShapeDtypeStruct(x.shape, F32), jax.ShapeDtypeStruct(across, F32)],
        in_specs=[ANY] * 5,
        out_specs=[ANY] * 2,
        scratch_shapes=[pltpu.VMEM(across, F32), pltpu.SemaphoreType.DMA((2,))],
        input_output_aliases={0: 0},
        compiler_params=pltpu.CompilerParams(vmem_limit_bytes=VMEM_LIMIT),
        cost_estimate=pl.CostEstimate(flops=0, bytes_accessed=2_000_000, transcendentals=0),
        name="join",
    )(x, low, high, *beside)


SPANS = ((0, 1536), (1536, 1792))
TILE = 256
BY_ROWS = (((1,), (1,)), ((), ()))


def panel_loads(places, x_ref, pieces, x, panel, x_sem, sem):
    loads = []
    for number, (start, length) in enumerate(SPANS):
        span = pl.ds(start, length)
        copies = [pltpu.make_async_copy(x_ref.at[span], x.at[span], x_sem.at[number])]
        height = pieces[0].shape[0]
        slot = 0
        for piece in pieces:
            for at in range(0, piece.shape[0], height):
                rows = pl.ds(pl.multiple_of(places[slot], height), height)
                copies.append(
                    pltpu.make_async_copy(piece.at[pl.ds(at, height), span], panel.at[rows, span], sem.at[number, slot])
                )
                slot += 1
        loads.append(copies)
    for copies in loads:
        for copy in copies:
            copy.start()
    return loads


def coeffs_kernel(shares, width, places, x_ref, *refs):
    *pieces, out_ref, panel, x, x_sem, sem = refs
    loads = panel_loads(places, x_ref, pieces, x, panel, x_sem, sem)
    coeffs = gram = None
    for (start, length), copies in zip(SPANS, loads):
        for copy in copies:
            copy.wait()
        span = slice(start, start + length)
        high, low = split(panel[:, span])
        x_high, x_low = split(x[span, :])
        part = dot(
            jnp.concatenate([high, low, high], axis=1), jnp.concatenate([x_high, x_high, x_low], axis=0)
        )
        gram_part = dot(
            jnp.concatenate([high[width:], low[width:], high[width:]], axis=1),
            jnp.concatenate([high[:width], high[:width], low[:width]], axis=1),
            BY_ROWS,
        )
        coeffs = part if coeffs is None else coeffs + part
        gram = gram_part if gram is None else gram + gram_part
    a, b = 2 * width // shares, width // shares
    out_ref[:, :a, :] = coeffs.reshape(shares, a, -1)
    out_ref[:, a:, :] = gram.reshape(shares, b, -1)


SMEM_SPEC = pl.BlockSpec(memory_space=pltpu.SMEM)
VMEM_SPEC = pl.BlockSpec(memory_space=pltpu.VMEM)


def panel_coeffs(shares, places, x, pieces, width):
    rows, columns = x.shape
    return pl.pallas_call(
        functools.partial(coeffs_kernel, shares, width),
        out_shape=jax.ShapeDtypeStruct((shares, 3 * width // shares, columns), F32),
        in_specs=[SMEM_SPEC] + [ANY] * (1 + len(pieces)),
        out_specs=VMEM_SPEC,
        scratch_shapes=[
            pltpu.VMEM((2 * width, rows), F32),
            pltpu.VMEM(x.shape, F32),
            pltpu.SemaphoreType.DMA((2,)),
            pltpu.SemaphoreType.DMA((2, 8)),
        ],
        compiler_params=pltpu.CompilerParams(vmem_limit_bytes=VMEM_LIMIT),
        cost_estimate=pl.CostEstimate(flops=4_000_000_000, bytes_accessed=11_000_000, transcendentals=0),
        name="panel_coeffs",
    )(places, x, *pieces)


def update_kernel(places, sums_ref, t_ref, x_ref, *refs):
    *pieces, out_ref, panel, x, x_sem, sem, store_sem = refs
    loads = panel_loads(places, x_ref, pieces, x, panel, x_sem, sem)
    width = t_ref.shape[1]
    shares = sums_ref.shape[0]
    a = 2 * width // shares
    coeffs = sums_ref[:, :a, :].reshape(2 * width, -1)
    gram = sums_ref[:, a:, :].reshape(width, width)
    first = dot3(split(t_ref[0]), split(coeffs[:width]))
    rest = coeffs[width:] - dot3(split(gram), split(first))
    second = dot3(split(t_ref[1]), split(rest))
    high, low = split(jnp.concatenate([first, second], axis=0))
    right = jnp.concatenate([high, high, low], axis=0)
    stores = []
    for number, ((start, length), copies) in enumerate(zip(SPANS, loads)):
        for copy in copies:
            copy.wait()
        for at in range(start, start + length, TILE):
            span = slice(at, at + TILE)
            high, low = split(panel[:, span])
            high, low = high.T, low.T
            x[span, :] = x[span, :] - dot(jnp.concatenate([high, low, high], axis=1), right)
        span = pl.ds(start, length)
        stores.append(pltpu.make_async_copy(x.at[span], out_ref.at[span], store_sem.at[number]))
        stores[-1].start()
    for copy in stores:
        copy.wait()


def update(places, sums, t, x, pieces):
    rows = x.shape[0]
    return pl.pallas_call(
        update_kernel,
        out_shape=jax.ShapeDtypeStruct(x.shape, F32),
        in_specs=[SMEM_SPEC, VMEM_SPEC, VMEM_SPEC] + [ANY] * (1 + len(pieces)),
        out_specs=ANY,
        scratch_shapes=[
            pltpu.VMEM((2 * t.shape[1], rows), F32),
            pltpu.VMEM(x.shape, F32),
            pltpu.SemaphoreType.DMA((2,)),
            pltpu.SemaphoreType.DMA((2, 8)),
            pltpu.SemaphoreType.DMA((2,)),
        ],
        compiler_params=pltpu.CompilerParams(vmem_limit_bytes=VMEM_LIMIT),
        cost_estimate=pl.CostEstimate(flops=3_000_000_000, bytes_accessed=14_000_000, transcendentals=0),
        name="update",
    )(places, sums, t, x, *pieces)


def send(value, axis, steps):
    count = lax.axis_size(axis)
    return lax.ppermute(value, axis, [(i, (i + steps) % count) for i in range(count)])


def per_device(eigvecs, reflect_y, reflect_w, panel_v, panel_t):
    rows = ("z", "y")
    shares = lax.axis_size(rows)
    width = panel_t.shape[1]
    own = panel_v.T
    height = own.shape[0]

    from_left = send(own, "x", 1)
    from_right = send(own, "x", -1)
    for_below, for_above = edges(None, 0, eigvecs, reflect_y, reflect_w)
    above, below = send(for_below, rows, 1), send(for_above, rows, -1)
    twin_own = send(own, "core", 1)

    x = interior(0, eigvecs, reflect_y, reflect_w)
    x, for_below, for_above, duo, low, high = edges(
        0, 4, x, reflect_y, reflect_w, (above, below), (from_left, from_right, twin_own)
    )
    above, below = send(for_below, rows, 1), send(for_above, rows, -1)
    low = send(low, "x", 1)
    high = send(high, "x", -1)
    twin_duo = send(duo, "core", 1)

    x = interior(4, x, reflect_y, reflect_w)
    x, across = join(x, low, high, above, below)
    twin_across = send(across, "core", 1)
    (x,) = edges(4, None, x, reflect_y, reflect_w, (above, below))

    pieces = [own, twin_own, duo, twin_duo, across, twin_across]
    at_x, at_core = lax.axis_index("x"), lax.axis_index("core")
    places = []
    for shifts in ((0,), (-1, 1), (2,)):
        for twin in (0, 1):
            for shift in shifts:
                col = (at_x + shift) % 4 * 2 + (at_core + twin) % 2
                places.append(col * height)
    places = jnp.stack(places).astype(jnp.int32)

    sums = panel_coeffs(shares, places, x, pieces, width)
    mine = jnp.sum(lax.all_to_all(sums, rows, 0, 0), axis=0)
    sums = lax.all_to_all(jnp.broadcast_to(mine[None], sums.shape), rows, 0, 0)
    return update(places, sums, panel_t, x, pieces)


def solution(mesh):
    z, y, x, core = 8, 4, 4, 2
    fine = Mesh(mesh.devices.reshape(z, y, x, core), ("z", "y", "x", "core"))
    row, col = ("z", "y"), ("x", "core")
    return jax.shard_map(
        per_device,
        mesh=fine,
        in_specs=(
            P(row, col),
            P(None, row, None, None),
            P(None, row, None, None),
            P(row, col),
            P(),
        ),
        out_specs=P(row, col),
        check_vma=False,
    )
```

```python
import functools

import jax
import jax.numpy as jnp
from jax import lax
from jax.experimental import pallas as pl
from jax.experimental.pallas import tpu as pltpu
from jax.sharding import Mesh, PartitionSpec as P

HALO = 128
EDGE = 256
PARTS = 3
GROUP = 9
ANY = pl.BlockSpec(memory_space=pl.ANY)
VMEM_SPEC = pl.BlockSpec(memory_space=pltpu.VMEM)
F32 = jnp.float32
BF16 = jnp.bfloat16
MIB = 1024 * 1024
INTERIOR_VMEM = 48 * MIB
EDGE_VMEM = 44 * MIB
COEFFS_VMEM = 40 * MIB
UPDATE_VMEM = 44 * MIB


def split(value):
    high = value.astype(BF16)
    low = (value - high.astype(F32)).astype(BF16)
    return high, low


def dot(left, right, dims=(((1,), (0,)), ((), ()))):
    return lax.dot_general(left, right, dims, preferred_element_type=F32)


def dot3(left, right, dims=(((1,), (0,)), ((), ()))):
    left_high, left_low = left
    right_high, right_low = right
    return (
        dot(left_high, right_low, dims) + dot(left_low, right_high, dims) + dot(left_high, right_high, dims)
    )


def band_steps(blocks):
    projected = []
    for z, y, _ in blocks:
        z_high, z_low = split(z)
        y_high, y_low = split(y)
        left = jnp.concatenate(
            [jnp.concatenate([y_high, y_high], axis=1), jnp.concatenate([y_low, y_low], axis=1)], axis=0
        )
        both = dot(left, jnp.concatenate([z_high, z_low], axis=0))
        half = y.shape[0]
        projected.append(both[:half] + both[half:])
    out = []
    for (z, _, w), p in zip(blocks, projected):
        p_high, p_low = split(p)
        w_high, w_low = split(w)
        turned = jnp.concatenate([w_high, w_low], axis=0).T
        left = jnp.concatenate([turned, turned], axis=1)
        out.append(z - dot(left, jnp.concatenate([p_high, p_high, p_low, p_low], axis=0)))
    return out


def interior_kernel(base, x_ref, y_ref, w_ref, x, y, w, first_sem, sweep_sem):
    windows = y.shape[1]
    cuts = [windows * part // PARTS for part in range(PARTS + 1)]
    first, later = [], []
    for part in range(PARTS):
        start, number = cuts[part], cuts[part + 1] - cuts[part]
        span = pl.ds(start * 128, number * 128)
        some = pl.ds(start, number)
        copies = [
            pltpu.make_async_copy(y_ref.at[base, some], y.at[0, some], first_sem.at[1, part]),
            pltpu.make_async_copy(w_ref.at[base, some], w.at[0, some], first_sem.at[2, part]),
        ]
        if base == 0:
            copies.append(pltpu.make_async_copy(x_ref.at[span], x.at[span], first_sem.at[0, part]))
        first.append(copies)
    for s in range(1, 4):
        later.append(
            (
                pltpu.make_async_copy(y_ref.at[base + s], y.at[s], sweep_sem.at[0, s]),
                pltpu.make_async_copy(w_ref.at[base + s], w.at[s], sweep_sem.at[1, s]),
            )
        )
    for copies in first + later:
        for copy in copies:
            copy.start()

    def run(s, start, stop):
        rows_of = [pl.ds(v * 128 + 64 * (s % 2), 128) for v in range(start, stop)]
        blocks = [(x[at, :], y[s, v], w[s, v]) for at, v in zip(rows_of, range(start, stop))]
        for at, value in zip(rows_of, band_steps(blocks)):
            x[at, :] = value

    for part in range(PARTS):
        for copy in first[part]:
            copy.wait()
        run(0, cuts[part], cuts[part + 1])
    for s in range(1, 4):
        for copy in later[s - 1]:
            copy.wait()
        begin, end = s // 2, s // 2 + windows - s
        for start in range(begin, end, GROUP):
            run(s, start, min(start + GROUP, end))


def interior(base, x, y, w):
    return pl.pallas_call(
        functools.partial(interior_kernel, base),
        out_shape=jax.ShapeDtypeStruct(x.shape, F32),
        in_specs=[VMEM_SPEC if base else ANY, ANY, ANY],
        out_specs=VMEM_SPEC,
        scratch_shapes=[
            pltpu.VMEM((4,) + y.shape[1:], F32),
            pltpu.VMEM((4,) + w.shape[1:], F32),
            pltpu.SemaphoreType.DMA((3, PARTS)),
            pltpu.SemaphoreType.DMA((2, 4)),
        ],
        input_output_aliases={0: 0} if base else {},
        compiler_params=pltpu.CompilerParams(vmem_limit_bytes=INTERIOR_VMEM),
        cost_estimate=pl.CostEstimate(flops=10_000_000_000, bytes_accessed=14_000_000, transcendentals=0),
        name=f"interior{base}",
    )(x, y, w)


def prepare_plan(base, last):
    return [
        [
            (0, 128, "own", (base, 0)),
            (0, 256, "own", (base, 1)),
            (1, 0, "own", (base, last - 1)),
            (1, 128, "own", (base, last)),
        ],
        [(0, 192, "own", (base + 1, 0)), (1, 64, "own", (base + 1, last - 1))],
    ]


def finish_plan(base, last):
    return [
        [(0, 64, "above", 0), (1, 192, "own", (base + 1, last))],
        [
            (0, 0, "above", 1),
            (0, 128, "own", (base + 2, 0)),
            (1, 128, "own", (base + 2, last)),
            (1, 256, "below", 0),
        ],
        [
            (0, 64, "above", 2),
            (0, 192, "own", (base + 3, 0)),
            (1, 64, "own", (base + 3, last - 1)),
            (1, 192, "own", (base + 3, last)),
        ],
    ]


def sent_reflectors(base, last):
    return [(base + 1, last), (base + 2, last), (base + 3, last)], [(base + 2, 0)]


def bundles(last):
    return [
        jax.ShapeDtypeStruct((2 * HALO + 2 * 64 * len(windows), 128), F32) for windows in sent_reflectors(0, last)
    ]


def edge_kernel(finish, prepare, last, *refs):
    refs = list(refs)
    take = lambda number: [refs.pop(0) for _ in range(number)]
    x_ref, y_ref, w_ref = take(3)
    above_ref = below_ref = None
    if finish is not None:
        above_ref, below_ref = take(2)
    if finish is not None:
        (out_ref,) = take(1)
    if prepare is not None:
        bundle_refs = take(2)
    side, y, w, sem = refs
    rows = x_ref.shape[0]
    used = [0]

    def copy(source, target):
        used[0] += 1
        return pltpu.make_async_copy(source, target, sem.at[used[0] - 1])

    def start(copies):
        for one in copies:
            one.start()

    def wait(copies):
        for one in copies:
            one.wait()

    loads = []
    if finish is None:
        loads = [
            copy(x_ref.at[pl.ds(0, EDGE)], side.at[0, pl.ds(HALO, EDGE)]),
            copy(x_ref.at[pl.ds(rows - EDGE, EDGE)], side.at[1, pl.ds(0, EDGE)]),
        ]
    else:
        side[0, pl.ds(HALO, EDGE), :] = x_ref[pl.ds(0, EDGE), :]
        side[1, pl.ds(0, EDGE), :] = x_ref[pl.ds(rows - EDGE, EDGE), :]
        for j in range(2):
            part, lanes = pl.ds(j * HALO, HALO), pl.ds(j * 128, 128)
            loads.append(copy(above_ref.at[part], side.at[0, pl.ds(0, HALO), lanes]))
            loads.append(copy(below_ref.at[part], side.at[1, pl.ds(EDGE, HALO), lanes]))
    start(loads)

    stages = []
    if finish is not None:
        stages += finish_plan(finish, last)
    if prepare is not None:
        stages += prepare_plan(prepare, last)
    slot = 0
    slots, waits = [], []
    for steps in stages:
        mine, copies = [], []
        for _, _, source, index in steps:
            if source == "own":
                y_source, w_source = y_ref.at[index], w_ref.at[index]
            else:
                ref = above_ref if source == "above" else below_ref
                height = (ref.shape[0] - 2 * HALO) // 2
                y_source = ref.at[pl.ds(2 * HALO + 64 * index, 64)]
                w_source = ref.at[pl.ds(2 * HALO + height + 64 * index, 64)]
            copies += [copy(y_source, y.at[slot]), copy(w_source, w.at[slot])]
            mine.append(slot)
            slot += 1
        start(copies)
        slots.append(mine)
        waits.append(copies)
    passing, sending = [], []
    if prepare is not None:
        for windows, out in zip(sent_reflectors(prepare, last), bundle_refs):
            at = 2 * HALO
            for index in windows:
                passing += [copy(y_ref.at[index], y.at[slot]), copy(w_ref.at[index], w.at[slot])]
                sending += [
                    copy(y.at[slot], out.at[pl.ds(at, 64)]),
                    copy(w.at[slot], out.at[pl.ds(at + 64 * len(windows), 64)]),
                ]
                slot += 1
                at += 64
    start(passing)
    wait(loads)

    def stage(number):
        wait(waits[number])
        blocks = [
            (side[which, pl.ds(row, 128), :], y[slots[number][j]], w[slots[number][j]])
            for j, (which, row, _, _) in enumerate(stages[number])
        ]
        for (which, row, _, _), value in zip(stages[number], band_steps(blocks)):
            side[which, pl.ds(row, 128), :] = value

    stores = []
    first = 0
    if finish is not None:
        first = 3
        for number in range(first):
            stage(number)
        out_ref[pl.ds(0, EDGE), :] = side[0, pl.ds(HALO, EDGE), :]
        out_ref[pl.ds(rows - EDGE, EDGE), :] = side[1, pl.ds(0, EDGE), :]
    wait(passing)
    start(sending)
    if prepare is not None:
        for number in range(first, first + 2):
            stage(number)
        for j in range(2):
            part, lanes = pl.ds(j * HALO, HALO), pl.ds(j * 128, 128)
            stores.append(copy(side.at[1, pl.ds(EDGE - HALO, HALO), lanes], bundle_refs[0].at[part]))
            stores.append(copy(side.at[0, pl.ds(HALO, HALO), lanes], bundle_refs[1].at[part]))
        start(stores)
    wait(stores + sending)


def edges(finish, prepare, x, y, w, halos=()):
    last = y.shape[1] - 1
    out_shape = []
    if finish is not None:
        out_shape.append(jax.ShapeDtypeStruct(x.shape, F32))
    if prepare is not None:
        out_shape += bundles(last)
    in_vmem = VMEM_SPEC if finish is not None else ANY
    return pl.pallas_call(
        functools.partial(edge_kernel, finish, prepare, last),
        out_shape=out_shape,
        in_specs=[in_vmem] + [ANY] * (2 + len(halos)),
        out_specs=[in_vmem] + [ANY] * (len(out_shape) - 1),
        scratch_shapes=[
            pltpu.VMEM((2, HALO + EDGE, x.shape[1]), F32),
            pltpu.VMEM((20,) + y.shape[2:], F32),
            pltpu.VMEM((20,) + w.shape[2:], F32),
            pltpu.SemaphoreType.DMA((80,)),
        ],
        input_output_aliases={} if finish is None else {0: 0},
        compiler_params=pltpu.CompilerParams(vmem_limit_bytes=EDGE_VMEM if finish is not None else 63 * MIB),
        cost_estimate=pl.CostEstimate(flops=1_500_000_000, bytes_accessed=3_000_000, transcendentals=0),
        name="edges",
    )(x, y, w, *halos)


def relay_kernel(left_ref, right_ref, own_ref, after_ref, duo_ref, low_ref, high_ref, duo, sem):
    height = left_ref.shape[0]
    half = height // 2
    left = pltpu.make_async_copy(left_ref, duo.at[pl.ds(0, height)], sem.at[0])
    right = pltpu.make_async_copy(right_ref, duo.at[pl.ds(height, height)], sem.at[1])
    left.start()
    right.start()
    left.wait()
    low = pltpu.make_async_copy(duo.at[pl.ds(0, half)], low_ref, sem.at[2])
    low.start()
    right.wait()
    high = pltpu.make_async_copy(duo.at[pl.ds(height + half, half)], high_ref, sem.at[3])
    high.start()
    both = pltpu.make_async_copy(duo, duo_ref, sem.at[4])
    both.start()
    low.wait()
    high.wait()
    both.wait()


def relay(left, right, *after):
    height, rows = left.shape
    return pl.pallas_call(
        relay_kernel,
        out_shape=[jax.ShapeDtypeStruct((part, rows), F32) for part in (2 * height, height // 2, height // 2)],
        in_specs=[ANY] * 4,
        out_specs=[ANY] * 3,
        scratch_shapes=[pltpu.VMEM((2 * height, rows), F32), pltpu.SemaphoreType.DMA((5,))],
        compiler_params=pltpu.CompilerParams(vmem_limit_bytes=EDGE_VMEM),
        cost_estimate=pl.CostEstimate(flops=0, bytes_accessed=5_000_000, transcendentals=0),
        name="relay",
    )(left, right, *after)


TILE = 256
BY_ROWS = (((1,), (1,)), ((), ()))


def spans(rows, number):
    tiles = rows // TILE
    cuts = [tiles * i // number * TILE for i in range(number + 1)]
    return [(start, stop - start) for start, stop in zip(cuts, cuts[1:])]


def stacked3(left, right, dims=(((1,), (0,)), ((), ()))):
    (left_high, left_low), (right_high, right_low) = left, right
    rows = left_high.shape[0]
    both = dot(jnp.concatenate([left_high, left_low], axis=0), right_high, dims)
    return both[:rows] + both[rows:] + dot(left_high, right_low, dims)


def panel_places(height):
    at_x, at_core = lax.axis_index("x"), lax.axis_index("core")
    places = []
    for parts in (((0, 0),), ((-1, 0), (1, 0)), ((2, 0),), ((2, height // 2),)):
        for twin in (0, 1):
            for shift, skip in parts:
                col = lax.rem(at_x + 4 + shift, 4) * 2 + lax.rem(at_core + twin, 2)
                places.append(col * height + skip)
    return places


def coeffs_kernel(shares, width, x_ref, t_ref, *refs):
    *pieces, out_ref, panel_ref, t, panel, t_sem, sem = refs
    total = x_ref.shape[0]
    t_load = pltpu.make_async_copy(t_ref, t, t_sem.at[0])
    t_load.start()
    parts = spans(x_ref.shape[0], 2)
    height = pieces[0].shape[0]
    places = panel_places(height)
    loads = []
    for number, (start, length) in enumerate(parts):
        span = pl.ds(start, length)
        copies = []
        for piece in pieces:
            step = min(height, piece.shape[0])
            for at in range(0, piece.shape[0], step):
                rows = pl.ds(pl.multiple_of(places[len(copies)], step), step)
                copies.append(
                    pltpu.make_async_copy(
                        piece.at[pl.ds(at, step), span], panel.at[rows, span], sem.at[number, len(copies)]
                    )
                )
        loads.append(copies)
    for copies in loads:
        for copy in copies:
            copy.start()
    coeffs = gram = None
    stores = []
    for number, ((start, length), copies) in enumerate(zip(parts, loads)):
        for copy in copies:
            copy.wait()
        span = pl.ds(start, length)
        stores.append(pltpu.make_async_copy(panel.at[:, span], panel_ref.at[:, span], sem.at[number, 10]))
        stores[-1].start()
        span = slice(start, start + length)
        high, low = split(panel[:, span])
        part = stacked3((high, low), split(x_ref[span, :]))
        gram_part = stacked3((high[width:], low[width:]), (high[:width], low[:width]), BY_ROWS)
        coeffs = part if coeffs is None else coeffs + part
        gram = gram_part if gram is None else gram + gram_part
    a, b = 2 * width // shares, width // shares
    out_ref[:, :a, :] = coeffs.reshape(shares, a, -1)
    out_ref[:, a:, :] = gram.reshape(shares, b, -1)
    t_load.wait()
    for i in range(2):
        beside = panel_ref.at[pl.ds(i * width, width), pl.ds(total, width)]
        stores.append(pltpu.make_async_copy(t.at[i], beside, t_sem.at[i]))
        stores[-1].start()
    for copy in stores:
        copy.wait()


def panel_coeffs(shares, x, t, pieces):
    width = t.shape[1]
    return pl.pallas_call(
        functools.partial(coeffs_kernel, shares, width),
        out_shape=[
            jax.ShapeDtypeStruct((shares, 3 * width // shares, x.shape[1]), F32),
            jax.ShapeDtypeStruct((2 * width, x.shape[0] + width), F32),
        ],
        in_specs=[VMEM_SPEC] + [ANY] * (1 + len(pieces)),
        out_specs=[VMEM_SPEC, ANY],
        scratch_shapes=[
            pltpu.VMEM(t.shape, F32),
            pltpu.VMEM((2 * width, x.shape[0]), F32),
            pltpu.SemaphoreType.DMA((2,)),
            pltpu.SemaphoreType.DMA((2, 11)),
        ],
        compiler_params=pltpu.CompilerParams(vmem_limit_bytes=COEFFS_VMEM),
        cost_estimate=pl.CostEstimate(flops=4_000_000_000, bytes_accessed=11_000_000, transcendentals=0),
        name="panel_coeffs",
    )(x, t, *pieces)


def update_kernel(width, sums_ref, x_ref, panel_ref, out_ref, panel, stage, t_sem, sem):
    rows = stage.shape[0]
    parts = spans(rows, 4)
    span = pl.ds(rows, width)
    t_load = pltpu.make_async_copy(panel_ref.at[:, span], panel.at[:, span], t_sem)
    t_load.start()
    loads = []
    for number, (start, length) in enumerate(parts):
        span = pl.ds(start, length)
        loads.append(pltpu.make_async_copy(panel_ref.at[:, span], panel.at[:, span], sem.at[0, number]))
        loads[-1].start()
    shares = sums_ref.shape[0]
    a = 2 * width // shares
    coeffs = sums_ref[:, :a, :].reshape(2 * width, -1)
    gram = sums_ref[:, a:, :].reshape(width, width)
    t_load.wait()
    t = panel[:, rows:]
    first = dot3(split(t[:width]), split(coeffs[:width]))
    rest = coeffs[width:] - dot3(split(gram), split(first))
    second = dot3(split(t[width:]), split(rest))
    right = split(jnp.concatenate([first, second], axis=0))
    stores = []
    for number, (start, length) in enumerate(parts):
        loads[number].wait()
        for at in range(start, start + length, TILE):
            span = slice(at, at + TILE)
            high, low = split(panel[:, span])
            stage[span, :] = x_ref[span, :] - stacked3((high.T, low.T), right)
        span = pl.ds(start, length)
        stores.append(pltpu.make_async_copy(stage.at[span], out_ref.at[span], sem.at[1, number]))
        stores[-1].start()
    for copy in stores:
        copy.wait()


def update(sums, x, panel, width):
    return pl.pallas_call(
        functools.partial(update_kernel, width),
        out_shape=jax.ShapeDtypeStruct(x.shape, F32),
        in_specs=[VMEM_SPEC, VMEM_SPEC, ANY],
        out_specs=ANY,
        scratch_shapes=[
            pltpu.VMEM(panel.shape, F32),
            pltpu.VMEM(x.shape, F32),
            pltpu.SemaphoreType.DMA,
            pltpu.SemaphoreType.DMA((2, 4)),
        ],
        compiler_params=pltpu.CompilerParams(vmem_limit_bytes=UPDATE_VMEM),
        cost_estimate=pl.CostEstimate(flops=3_000_000_000, bytes_accessed=14_000_000, transcendentals=0),
        name="update",
    )(sums, x, panel)


def send(value, axis, steps):
    count = lax.axis_size(axis)
    return lax.ppermute(value, axis, [(i, (i + steps) % count) for i in range(count)])


def per_device(eigvecs, reflect_y, reflect_w, panel_v, panel_t):
    rows = ("z", "y")
    shares = lax.axis_size(rows)
    own = panel_v.T

    from_left = send(own, "x", 1)
    from_right = send(own, "x", -1)
    for_below, for_above = edges(None, 0, eigvecs, reflect_y, reflect_w)
    above, below = send(for_below, rows, 1), send(for_above, rows, -1)
    twin_own = send(own, "core", 1)

    x = interior(0, eigvecs, reflect_y, reflect_w)
    x, for_below, for_above = edges(0, 4, x, reflect_y, reflect_w, (above, below))
    above, below = send(for_below, rows, 1), send(for_above, rows, -1)
    duo, low, high = relay(from_left, from_right, twin_own, for_below)
    low = send(low, "x", 1)
    high = send(high, "x", -1)
    twin_duo = send(duo, "core", 1)

    x = interior(4, x, reflect_y, reflect_w)
    x, low, high, above, below = lax.optimization_barrier((x, low, high, above, below))
    twin_low, twin_high = send(low, "core", 1), send(high, "core", 1)
    (x,) = edges(4, None, x, reflect_y, reflect_w, (above, below))

    pieces = [own, twin_own, duo, twin_duo, low, twin_low, high, twin_high]
    sums, panel = panel_coeffs(shares, x, panel_t, pieces)
    mine = jnp.sum(lax.all_to_all(sums, rows, 0, 0), axis=0)
    sums = lax.all_to_all(jnp.broadcast_to(mine[None], sums.shape), rows, 0, 0)
    return update(sums, x, panel, panel_t.shape[1])


def solution(mesh):
    z, y, x, core = 8, 4, 4, 2
    fine = Mesh(mesh.devices.reshape(z, y, x, core), ("z", "y", "x", "core"))
    row, col = ("z", "y"), ("x", "core")
    return jax.shard_map(
        per_device,
        mesh=fine,
        in_specs=(
            P(row, col),
            P(None, row, None, None),
            P(None, row, None, None),
            P(row, col),
            P(),
        ),
        out_specs=P(row, col),
        check_vma=False,
    )
```

```python
import functools

import jax
import jax.numpy as jnp
from jax import lax
from jax.experimental import pallas as pl
from jax.experimental.pallas import tpu as pltpu
from jax.sharding import Mesh, PartitionSpec as P

HALO = 128
EDGE = 256
PARTS = 3
GROUP = 9
ANY = pl.BlockSpec(memory_space=pl.ANY)
VMEM_SPEC = pl.BlockSpec(memory_space=pltpu.VMEM)
F32 = jnp.float32
BF16 = jnp.bfloat16
MIB = 1024 * 1024
INTERIOR_VMEM = 48 * MIB
EDGE_VMEM = 44 * MIB
COEFFS_VMEM = 40 * MIB
UPDATE_VMEM = 44 * MIB


def split(value):
    high = value.astype(BF16)
    low = (value - high.astype(F32)).astype(BF16)
    return high, low


def dot(left, right, dims=(((1,), (0,)), ((), ()))):
    return lax.dot_general(left, right, dims, preferred_element_type=F32)


def dot3(left, right, dims=(((1,), (0,)), ((), ()))):
    left_high, left_low = left
    right_high, right_low = right
    return (
        dot(left_high, right_low, dims) + dot(left_low, right_high, dims) + dot(left_high, right_high, dims)
    )


def band_steps(blocks):
    projected = []
    for z, y, _ in blocks:
        z_high, z_low = split(z)
        y_high, y_low = split(y)
        left = jnp.concatenate(
            [jnp.concatenate([y_high, y_high], axis=1), jnp.concatenate([y_low, y_low], axis=1)], axis=0
        )
        both = dot(left, jnp.concatenate([z_high, z_low], axis=0))
        half = y.shape[0]
        projected.append(both[:half] + both[half:])
    out = []
    for (z, _, w), p in zip(blocks, projected):
        p_high, p_low = split(p)
        w_high, w_low = split(w)
        turned = jnp.concatenate([w_high, w_low], axis=0).T
        left = jnp.concatenate([turned, turned], axis=1)
        out.append(z - dot(left, jnp.concatenate([p_high, p_high, p_low, p_low], axis=0)))
    return out


def interior_kernel(base, x_ref, y_ref, w_ref, x, y, w, first_sem, sweep_sem):
    windows = y.shape[1]
    cuts = [windows * part // PARTS for part in range(PARTS + 1)]
    first, later = [], []
    for part in range(PARTS):
        start, number = cuts[part], cuts[part + 1] - cuts[part]
        span = pl.ds(start * 128, number * 128)
        some = pl.ds(start, number)
        copies = [
            pltpu.make_async_copy(y_ref.at[base, some], y.at[0, some], first_sem.at[1, part]),
            pltpu.make_async_copy(w_ref.at[base, some], w.at[0, some], first_sem.at[2, part]),
        ]
        if base == 0:
            copies.append(pltpu.make_async_copy(x_ref.at[span], x.at[span], first_sem.at[0, part]))
        first.append(copies)
    for s in range(1, 4):
        later.append(
            (
                pltpu.make_async_copy(y_ref.at[base + s], y.at[s], sweep_sem.at[0, s]),
                pltpu.make_async_copy(w_ref.at[base + s], w.at[s], sweep_sem.at[1, s]),
            )
        )
    for copies in first + later:
        for copy in copies:
            copy.start()

    def run(s, start, stop):
        rows_of = [pl.ds(v * 128 + 64 * (s % 2), 128) for v in range(start, stop)]
        blocks = [(x[at, :], y[s, v], w[s, v]) for at, v in zip(rows_of, range(start, stop))]
        for at, value in zip(rows_of, band_steps(blocks)):
            x[at, :] = value

    for part in range(PARTS):
        for copy in first[part]:
            copy.wait()
        run(0, cuts[part], cuts[part + 1])
    for s in range(1, 4):
        for copy in later[s - 1]:
            copy.wait()
        begin, end = s // 2, s // 2 + windows - s
        for start in range(begin, end, GROUP):
            run(s, start, min(start + GROUP, end))


def interior(base, x, y, w):
    return pl.pallas_call(
        functools.partial(interior_kernel, base),
        out_shape=jax.ShapeDtypeStruct(x.shape, F32),
        in_specs=[VMEM_SPEC if base else ANY, ANY, ANY],
        out_specs=VMEM_SPEC,
        scratch_shapes=[
            pltpu.VMEM((4,) + y.shape[1:], F32),
            pltpu.VMEM((4,) + w.shape[1:], F32),
            pltpu.SemaphoreType.DMA((3, PARTS)),
            pltpu.SemaphoreType.DMA((2, 4)),
        ],
        input_output_aliases={0: 0} if base else {},
        compiler_params=pltpu.CompilerParams(vmem_limit_bytes=INTERIOR_VMEM),
        cost_estimate=pl.CostEstimate(flops=10_000_000_000, bytes_accessed=14_000_000, transcendentals=0),
        name=f"interior{base}",
    )(x, y, w)


def prepare_plan(base, last):
    return [
        [
            (0, 128, "own", (base, 0)),
            (0, 256, "own", (base, 1)),
            (1, 0, "own", (base, last - 1)),
            (1, 128, "own", (base, last)),
        ],
        [(0, 192, "own", (base + 1, 0)), (1, 64, "own", (base + 1, last - 1))],
    ]


def finish_plan(base, last):
    return [
        [(0, 64, "above", 0), (1, 192, "own", (base + 1, last))],
        [
            (0, 0, "above", 1),
            (0, 128, "own", (base + 2, 0)),
            (1, 128, "own", (base + 2, last)),
            (1, 256, "below", 0),
        ],
        [
            (0, 64, "above", 2),
            (0, 192, "own", (base + 3, 0)),
            (1, 64, "own", (base + 3, last - 1)),
            (1, 192, "own", (base + 3, last)),
        ],
    ]


def sent_reflectors(base, last):
    return [(base + 1, last), (base + 2, last), (base + 3, last)], [(base + 2, 0)]


def bundles(last):
    return [
        jax.ShapeDtypeStruct((2 * HALO + 2 * 64 * len(windows), 128), F32) for windows in sent_reflectors(0, last)
    ]


def edge_kernel(finish, prepare, last, *refs):
    refs = list(refs)
    take = lambda number: [refs.pop(0) for _ in range(number)]
    x_ref, y_ref, w_ref = take(3)
    above_ref = below_ref = None
    if finish is not None:
        above_ref, below_ref = take(2)
    if finish is not None:
        (out_ref,) = take(1)
    if prepare is not None:
        bundle_refs = take(2)
    side, y, w, sem = refs
    rows = x_ref.shape[0]
    used = [0]

    def copy(source, target):
        used[0] += 1
        return pltpu.make_async_copy(source, target, sem.at[used[0] - 1])

    def start(copies):
        for one in copies:
            one.start()

    def wait(copies):
        for one in copies:
            one.wait()

    loads = []
    if finish is None:
        loads = [
            copy(x_ref.at[pl.ds(0, EDGE)], side.at[0, pl.ds(HALO, EDGE)]),
            copy(x_ref.at[pl.ds(rows - EDGE, EDGE)], side.at[1, pl.ds(0, EDGE)]),
        ]
    else:
        side[0, pl.ds(HALO, EDGE), :] = x_ref[pl.ds(0, EDGE), :]
        side[1, pl.ds(0, EDGE), :] = x_ref[pl.ds(rows - EDGE, EDGE), :]
        for j in range(2):
            part, lanes = pl.ds(j * HALO, HALO), pl.ds(j * 128, 128)
            loads.append(copy(above_ref.at[part], side.at[0, pl.ds(0, HALO), lanes]))
            loads.append(copy(below_ref.at[part], side.at[1, pl.ds(EDGE, HALO), lanes]))
    start(loads)

    stages = []
    if finish is not None:
        stages += finish_plan(finish, last)
    if prepare is not None:
        stages += prepare_plan(prepare, last)
    slot = 0
    slots, waits = [], []
    for steps in stages:
        mine, copies = [], []
        for _, _, source, index in steps:
            if source == "own":
                y_source, w_source = y_ref.at[index], w_ref.at[index]
            else:
                ref = above_ref if source == "above" else below_ref
                height = (ref.shape[0] - 2 * HALO) // 2
                y_source = ref.at[pl.ds(2 * HALO + 64 * index, 64)]
                w_source = ref.at[pl.ds(2 * HALO + height + 64 * index, 64)]
            copies += [copy(y_source, y.at[slot]), copy(w_source, w.at[slot])]
            mine.append(slot)
            slot += 1
        start(copies)
        slots.append(mine)
        waits.append(copies)
    passing, sending = [], []
    if prepare is not None:
        for windows, out in zip(sent_reflectors(prepare, last), bundle_refs):
            at = 2 * HALO
            for index in windows:
                passing += [copy(y_ref.at[index], y.at[slot]), copy(w_ref.at[index], w.at[slot])]
                sending += [
                    copy(y.at[slot], out.at[pl.ds(at, 64)]),
                    copy(w.at[slot], out.at[pl.ds(at + 64 * len(windows), 64)]),
                ]
                slot += 1
                at += 64
    start(passing)
    wait(loads)

    def stage(number):
        wait(waits[number])
        blocks = [
            (side[which, pl.ds(row, 128), :], y[slots[number][j]], w[slots[number][j]])
            for j, (which, row, _, _) in enumerate(stages[number])
        ]
        for (which, row, _, _), value in zip(stages[number], band_steps(blocks)):
            side[which, pl.ds(row, 128), :] = value

    stores = []
    first = 0
    if finish is not None:
        first = 3
        for number in range(first):
            stage(number)
        out_ref[pl.ds(0, EDGE), :] = side[0, pl.ds(HALO, EDGE), :]
        out_ref[pl.ds(rows - EDGE, EDGE), :] = side[1, pl.ds(0, EDGE), :]
    wait(passing)
    start(sending)
    if prepare is not None:
        for number in range(first, first + 2):
            stage(number)
        for j in range(2):
            part, lanes = pl.ds(j * HALO, HALO), pl.ds(j * 128, 128)
            stores.append(copy(side.at[1, pl.ds(EDGE - HALO, HALO), lanes], bundle_refs[0].at[part]))
            stores.append(copy(side.at[0, pl.ds(HALO, HALO), lanes], bundle_refs[1].at[part]))
        start(stores)
    wait(stores + sending)


def edges(finish, prepare, x, y, w, halos=()):
    last = y.shape[1] - 1
    out_shape = []
    if finish is not None:
        out_shape.append(jax.ShapeDtypeStruct(x.shape, F32))
    if prepare is not None:
        out_shape += bundles(last)
    in_vmem = VMEM_SPEC if finish is not None else ANY
    return pl.pallas_call(
        functools.partial(edge_kernel, finish, prepare, last),
        out_shape=out_shape,
        in_specs=[in_vmem] + [ANY] * (2 + len(halos)),
        out_specs=[in_vmem] + [ANY] * (len(out_shape) - 1),
        scratch_shapes=[
            pltpu.VMEM((2, HALO + EDGE, x.shape[1]), F32),
            pltpu.VMEM((20,) + y.shape[2:], F32),
            pltpu.VMEM((20,) + w.shape[2:], F32),
            pltpu.SemaphoreType.DMA((80,)),
        ],
        input_output_aliases={} if finish is None else {0: 0},
        compiler_params=pltpu.CompilerParams(vmem_limit_bytes=EDGE_VMEM if finish is not None else 63 * MIB),
        cost_estimate=pl.CostEstimate(flops=1_500_000_000, bytes_accessed=3_000_000, transcendentals=0),
        name="edges",
    )(x, y, w, *halos)


def relay_kernel(left_ref, right_ref, own_ref, after_ref, trio_ref, low_ref, high_ref, trio, sem):
    height = left_ref.shape[0]
    half = height // 2
    left = pltpu.make_async_copy(left_ref, trio.at[pl.ds(height, height)], sem.at[0])
    right = pltpu.make_async_copy(right_ref, trio.at[pl.ds(2 * height, height)], sem.at[1])
    own = pltpu.make_async_copy(own_ref, trio.at[pl.ds(0, height)], sem.at[2])
    for copy in (left, right, own):
        copy.start()
    left.wait()
    low = pltpu.make_async_copy(trio.at[pl.ds(height, half)], low_ref, sem.at[3])
    low.start()
    right.wait()
    high = pltpu.make_async_copy(trio.at[pl.ds(2 * height + half, half)], high_ref, sem.at[4])
    high.start()
    own.wait()
    whole = pltpu.make_async_copy(trio, trio_ref, sem.at[5])
    whole.start()
    for copy in (low, high, whole):
        copy.wait()


def relay(left, right, own, after):
    height, rows = own.shape
    return pl.pallas_call(
        relay_kernel,
        out_shape=[jax.ShapeDtypeStruct((part, rows), F32) for part in (3 * height, height // 2, height // 2)],
        in_specs=[ANY] * 4,
        out_specs=[ANY] * 3,
        scratch_shapes=[pltpu.VMEM((3 * height, rows), F32), pltpu.SemaphoreType.DMA((6,))],
        compiler_params=pltpu.CompilerParams(vmem_limit_bytes=EDGE_VMEM),
        cost_estimate=pl.CostEstimate(flops=0, bytes_accessed=5_000_000, transcendentals=0),
        name="relay",
    )(left, right, own, after)


TILE = 256
BY_ROWS = (((1,), (1,)), ((), ()))


def spans(rows, number):
    tiles = rows // TILE
    cuts = [tiles * i // number * TILE for i in range(number + 1)]
    return [(start, stop - start) for start, stop in zip(cuts, cuts[1:])]


def stacked3(left, right, dims=(((1,), (0,)), ((), ()))):
    (left_high, left_low), (right_high, right_low) = left, right
    rows = left_high.shape[0]
    both = dot(jnp.concatenate([left_high, left_low], axis=0), right_high, dims)
    return both[:rows] + both[rows:] + dot(left_high, right_low, dims)


def panel_places(height):
    at_x, at_core = lax.axis_index("x"), lax.axis_index("core")
    places = []
    for parts in (((0, 0), (-1, 0), (1, 0)), ((2, 0),), ((2, height // 2),)):
        for twin in (0, 1):
            for shift, skip in parts:
                col = lax.rem(at_x + 4 + shift, 4) * 2 + lax.rem(at_core + twin, 2)
                places.append(col * height + skip)
    return places


def coeffs_kernel(shares, width, x_ref, t_ref, *refs):
    *pieces, out_ref, panel_ref, t, panel, t_sem, sem = refs
    total = x_ref.shape[0]
    half = width // 2
    t_load = pltpu.make_async_copy(t_ref, t, t_sem.at[0])
    t_load.start()
    parts = spans(x_ref.shape[0], 2)
    height = 2 * pieces[-1].shape[0]
    places = panel_places(height)
    loads = []
    for number, (start, length) in enumerate(parts):
        span = pl.ds(start, length)
        copies = []
        for piece in pieces:
            step = min(height, piece.shape[0])
            for at in range(0, piece.shape[0], step):
                rows = pl.ds(pl.multiple_of(places[len(copies)], step), step)
                copies.append(
                    pltpu.make_async_copy(
                        piece.at[pl.ds(at, step), span], panel.at[rows, span], sem.at[number, len(copies)]
                    )
                )
        loads.append(copies)
    for copies in loads:
        for copy in copies:
            copy.start()
    coeffs = gram = None
    stores = []
    t_load.wait()
    for i in range(2):
        beside = panel_ref.at[pl.ds(i * width, width), pl.ds(total, width)]
        stores.append(pltpu.make_async_copy(t.at[i], beside, t_sem.at[i]))
        stores[-1].start()
    for number, ((start, length), copies) in enumerate(zip(parts, loads)):
        for copy in copies:
            copy.wait()
        span = pl.ds(start, length)
        stores.append(pltpu.make_async_copy(panel.at[:, span], panel_ref.at[:, span], sem.at[number, 10]))
        stores[-1].start()
        span = slice(start, start + length)
        high, low = split(panel[:, span])
        part = stacked3((high, low), split(x_ref[span, :]))
        mine = split(panel[pl.ds(pl.multiple_of(lax.axis_index("core") * half, half), half), span])
        gram_part = stacked3((high[width:], low[width:]), mine, BY_ROWS)
        coeffs = part if coeffs is None else coeffs + part
        gram = gram_part if gram is None else gram + gram_part
    a = 2 * width // shares
    out_ref[:, :a, :] = coeffs[:, :half].reshape(shares, a, half)
    out_ref[:, a : 2 * a, :] = coeffs[:, half:].reshape(shares, a, half)
    out_ref[:, 2 * a :, :] = gram.reshape(shares, width // shares, half)
    for copy in stores:
        copy.wait()


def panel_coeffs(shares, x, t, pieces):
    width = t.shape[1]
    return pl.pallas_call(
        functools.partial(coeffs_kernel, shares, width),
        out_shape=[
            jax.ShapeDtypeStruct((shares, 5 * width // shares, width // 2), F32),
            jax.ShapeDtypeStruct((2 * width, x.shape[0] + width), F32),
        ],
        in_specs=[VMEM_SPEC] + [ANY] * (1 + len(pieces)),
        out_specs=[VMEM_SPEC, ANY],
        scratch_shapes=[
            pltpu.VMEM(t.shape, F32),
            pltpu.VMEM((2 * width, x.shape[0]), F32),
            pltpu.SemaphoreType.DMA((2,)),
            pltpu.SemaphoreType.DMA((2, 11)),
        ],
        compiler_params=pltpu.CompilerParams(vmem_limit_bytes=COEFFS_VMEM),
        cost_estimate=pl.CostEstimate(flops=4_000_000_000, bytes_accessed=11_000_000, transcendentals=0),
        name="panel_coeffs",
    )(x, t, *pieces)


def update_kernel(width, sums_ref, x_ref, panel_ref, twin_ref, out_ref, panel, stage, twin, t_sem, twin_sem, sem):
    rows = stage.shape[0]
    parts = spans(rows, 4)
    span = pl.ds(rows, width)
    t_load = pltpu.make_async_copy(panel_ref.at[:, span], panel.at[:, span], t_sem)
    t_load.start()
    a = 2 * width // sums_ref.shape[0]
    twin_load = pltpu.make_async_copy(twin_ref.at[:, pl.ds(2 * a, a // 2)], twin, twin_sem)
    twin_load.start()
    loads = []
    for number, (start, length) in enumerate(parts):
        span = pl.ds(start, length)
        loads.append(pltpu.make_async_copy(panel_ref.at[:, span], panel.at[:, span], sem.at[0, number]))
        loads[-1].start()
    half = width // 2
    whole = [sums_ref[:, i * a : (i + 1) * a, :].reshape(2 * width, half) for i in range(2)]
    coeffs = jnp.concatenate(whole, axis=1)
    t_load.wait()
    t = panel[:, rows:]
    first = dot3(split(t[:width]), split(coeffs[:width]))
    twin_load.wait()
    mine, other = sums_ref[:, 2 * a :, :].reshape(width, half), twin[...].reshape(width, half)
    is_first = lax.axis_index("core") == 0
    gram = jnp.concatenate([jnp.where(is_first, mine, other), jnp.where(is_first, other, mine)], axis=1)
    rest = coeffs[width:] - dot3(split(gram), split(first))
    second = dot3(split(t[width:]), split(rest))
    right = split(jnp.concatenate([first, second], axis=0))
    stores = []
    for number, (start, length) in enumerate(parts):
        loads[number].wait()
        for at in range(start, start + length, TILE):
            span = slice(at, at + TILE)
            high, low = split(panel[:, span])
            stage[span, :] = x_ref[span, :] - stacked3((high.T, low.T), right)
        span = pl.ds(start, length)
        stores.append(pltpu.make_async_copy(stage.at[span], out_ref.at[span], sem.at[1, number]))
        stores[-1].start()
    for copy in stores:
        copy.wait()


def update(sums, x, panel, twin, width):
    return pl.pallas_call(
        functools.partial(update_kernel, width),
        out_shape=jax.ShapeDtypeStruct(x.shape, F32),
        in_specs=[VMEM_SPEC, VMEM_SPEC, ANY, ANY],
        out_specs=ANY,
        scratch_shapes=[
            pltpu.VMEM(panel.shape, F32),
            pltpu.VMEM(x.shape, F32),
            pltpu.VMEM((sums.shape[0], width // sums.shape[0], width // 2), F32),
            pltpu.SemaphoreType.DMA,
            pltpu.SemaphoreType.DMA,
            pltpu.SemaphoreType.DMA((2, 4)),
        ],
        compiler_params=pltpu.CompilerParams(vmem_limit_bytes=UPDATE_VMEM),
        cost_estimate=pl.CostEstimate(flops=3_000_000_000, bytes_accessed=14_000_000, transcendentals=0),
        name="update",
    )(sums, x, panel, twin)


def send(value, axis, steps):
    count = lax.axis_size(axis)
    return lax.ppermute(value, axis, [(i, (i + steps) % count) for i in range(count)])


def per_device(eigvecs, reflect_y, reflect_w, panel_v, panel_t):
    rows = ("z", "y")
    shares = lax.axis_size(rows)
    own = panel_v.T

    from_left = send(own, "x", 1)
    from_right = send(own, "x", -1)
    for_below, for_above = edges(None, 0, eigvecs, reflect_y, reflect_w)
    above, below = send(for_below, rows, 1), send(for_above, rows, -1)

    x = interior(0, eigvecs, reflect_y, reflect_w)
    x, for_below, for_above = edges(0, 4, x, reflect_y, reflect_w, (above, below))
    trio, low, high = relay(from_left, from_right, own, for_below)
    low, high = send(low, "x", 1), send(high, "x", -1)
    above, below = send(for_below, rows, 1), send(for_above, rows, -1)
    twin_trio = send(trio, "core", 1)

    x = interior(4, x, reflect_y, reflect_w)
    x, low, high, above, below = lax.optimization_barrier((x, low, high, above, below))
    twin_low, twin_high = send(low, "core", 1), send(high, "core", 1)
    (x,) = edges(4, None, x, reflect_y, reflect_w, (above, below))

    pieces = [trio, twin_trio, low, twin_low, high, twin_high]
    sums, panel = panel_coeffs(shares, x, panel_t, pieces)
    mine = jnp.sum(lax.all_to_all(sums, rows, 0, 0), axis=0)
    sums = lax.all_to_all(jnp.broadcast_to(mine[None], sums.shape), rows, 0, 0)
    return update(sums, x, panel, send(sums, "core", 1), panel_t.shape[1])


def solution(mesh):
    z, y, x, core = 8, 4, 4, 2
    fine = Mesh(mesh.devices.reshape(z, y, x, core), ("z", "y", "x", "core"))
    row, col = ("z", "y"), ("x", "core")
    return jax.shard_map(
        per_device,
        mesh=fine,
        in_specs=(
            P(row, col),
            P(None, row, None, None),
            P(None, row, None, None),
            P(row, col),
            P(),
        ),
        out_specs=P(row, col),
        check_vma=False,
    )
```

```python
import functools

import jax
import jax.numpy as jnp
from jax import lax
from jax.experimental import pallas as pl
from jax.experimental.pallas import tpu as pltpu
from jax.sharding import Mesh, PartitionSpec as P

HALO = 128
EDGE = 256
PARTS = 3
GROUP = 9
ANY = pl.BlockSpec(memory_space=pl.ANY)
VMEM_SPEC = pl.BlockSpec(memory_space=pltpu.VMEM)
F32 = jnp.float32
BF16 = jnp.bfloat16
MIB = 1024 * 1024
INTERIOR_VMEM = 48 * MIB
EDGE_VMEM = 44 * MIB
COEFFS_VMEM = 40 * MIB
UPDATE_VMEM = 44 * MIB


def split(value):
    high = value.astype(BF16)
    low = (value - high.astype(F32)).astype(BF16)
    return high, low


def dot(left, right, dims=(((1,), (0,)), ((), ()))):
    return lax.dot_general(left, right, dims, preferred_element_type=F32)


def dot3(left, right, dims=(((1,), (0,)), ((), ()))):
    left_high, left_low = left
    right_high, right_low = right
    return (
        dot(left_high, right_low, dims) + dot(left_low, right_high, dims) + dot(left_high, right_high, dims)
    )


def band_steps(blocks):
    projected = []
    for z, y, _ in blocks:
        z_high, z_low = split(z)
        y_high, y_low = split(y)
        left = jnp.concatenate(
            [jnp.concatenate([y_high, y_high], axis=1), jnp.concatenate([y_low, y_low], axis=1)], axis=0
        )
        both = dot(left, jnp.concatenate([z_high, z_low], axis=0))
        half = y.shape[0]
        projected.append(both[:half] + both[half:])
    out = []
    for (z, _, w), p in zip(blocks, projected):
        p_high, p_low = split(p)
        w_high, w_low = split(w)
        turned = jnp.concatenate([w_high, w_low], axis=0).T
        left = jnp.concatenate([turned, turned], axis=1)
        out.append(z - dot(left, jnp.concatenate([p_high, p_high, p_low, p_low], axis=0)))
    return out


def interior_kernel(base, x_ref, y_ref, w_ref, x, y, w, first_sem, sweep_sem):
    windows = y.shape[1]
    cuts = [windows * part // PARTS for part in range(PARTS + 1)]
    first, later = [], []
    for part in range(PARTS):
        start, number = cuts[part], cuts[part + 1] - cuts[part]
        span = pl.ds(start * 128, number * 128)
        some = pl.ds(start, number)
        copies = [
            pltpu.make_async_copy(y_ref.at[base, some], y.at[0, some], first_sem.at[1, part]),
            pltpu.make_async_copy(w_ref.at[base, some], w.at[0, some], first_sem.at[2, part]),
        ]
        if base == 0:
            copies.append(pltpu.make_async_copy(x_ref.at[span], x.at[span], first_sem.at[0, part]))
        first.append(copies)
    for s in range(1, 4):
        later.append(
            (
                pltpu.make_async_copy(y_ref.at[base + s], y.at[s], sweep_sem.at[0, s]),
                pltpu.make_async_copy(w_ref.at[base + s], w.at[s], sweep_sem.at[1, s]),
            )
        )
    for copies in first + later:
        for copy in copies:
            copy.start()

    def run(s, start, stop):
        rows_of = [pl.ds(v * 128 + 64 * (s % 2), 128) for v in range(start, stop)]
        blocks = [(x[at, :], y[s, v], w[s, v]) for at, v in zip(rows_of, range(start, stop))]
        for at, value in zip(rows_of, band_steps(blocks)):
            x[at, :] = value

    for part in range(PARTS):
        for copy in first[part]:
            copy.wait()
        run(0, cuts[part], cuts[part + 1])
    for s in range(1, 4):
        for copy in later[s - 1]:
            copy.wait()
        begin, end = s // 2, s // 2 + windows - s
        for start in range(begin, end, GROUP):
            run(s, start, min(start + GROUP, end))


def interior(base, x, y, w):
    return pl.pallas_call(
        functools.partial(interior_kernel, base),
        out_shape=jax.ShapeDtypeStruct(x.shape, F32),
        in_specs=[VMEM_SPEC if base else ANY, ANY, ANY],
        out_specs=VMEM_SPEC,
        scratch_shapes=[
            pltpu.VMEM((4,) + y.shape[1:], F32),
            pltpu.VMEM((4,) + w.shape[1:], F32),
            pltpu.SemaphoreType.DMA((3, PARTS)),
            pltpu.SemaphoreType.DMA((2, 4)),
        ],
        input_output_aliases={0: 0} if base else {},
        compiler_params=pltpu.CompilerParams(vmem_limit_bytes=INTERIOR_VMEM),
        cost_estimate=pl.CostEstimate(flops=2_000_000_000, bytes_accessed=1_000_000, transcendentals=0),
        name=f"interior{base}",
    )(x, y, w)


def prepare_plan(base, last):
    return [
        [
            (0, 128, "own", (base, 0)),
            (0, 256, "own", (base, 1)),
            (1, 0, "own", (base, last - 1)),
            (1, 128, "own", (base, last)),
        ],
        [(0, 192, "own", (base + 1, 0)), (1, 64, "own", (base + 1, last - 1))],
    ]


def finish_plan(base, last):
    return [
        [(0, 64, "above", 0), (1, 192, "own", (base + 1, last))],
        [
            (0, 0, "above", 1),
            (0, 128, "own", (base + 2, 0)),
            (1, 128, "own", (base + 2, last)),
            (1, 256, "below", 0),
        ],
        [
            (0, 64, "above", 2),
            (0, 192, "own", (base + 3, 0)),
            (1, 64, "own", (base + 3, last - 1)),
            (1, 192, "own", (base + 3, last)),
        ],
    ]


def sent_reflectors(base, last):
    return [(base + 1, last), (base + 2, last), (base + 3, last)], [(base + 2, 0)]


def bundles(last):
    return [
        jax.ShapeDtypeStruct((2 * HALO + 2 * 64 * len(windows), 128), F32) for windows in sent_reflectors(0, last)
    ]


def edge_kernel(finish, prepare, last, *refs):
    refs = list(refs)
    take = lambda number: [refs.pop(0) for _ in range(number)]
    x_ref, y_ref, w_ref = take(3)
    above_ref = below_ref = None
    if finish is not None:
        above_ref, below_ref = take(2)
    if finish is not None:
        (out_ref,) = take(1)
    if prepare is not None:
        bundle_refs = take(2)
    side, y, w, sem = refs
    rows = x_ref.shape[0]
    used = [0]

    def copy(source, target):
        used[0] += 1
        return pltpu.make_async_copy(source, target, sem.at[used[0] - 1])

    def start(copies):
        for one in copies:
            one.start()

    def wait(copies):
        for one in copies:
            one.wait()

    loads = []
    if finish is None:
        loads = [
            copy(x_ref.at[pl.ds(0, EDGE)], side.at[0, pl.ds(HALO, EDGE)]),
            copy(x_ref.at[pl.ds(rows - EDGE, EDGE)], side.at[1, pl.ds(0, EDGE)]),
        ]
    else:
        side[0, pl.ds(HALO, EDGE), :] = x_ref[pl.ds(0, EDGE), :]
        side[1, pl.ds(0, EDGE), :] = x_ref[pl.ds(rows - EDGE, EDGE), :]
        for j in range(2):
            part, lanes = pl.ds(j * HALO, HALO), pl.ds(j * 128, 128)
            loads.append(copy(above_ref.at[part], side.at[0, pl.ds(0, HALO), lanes]))
            loads.append(copy(below_ref.at[part], side.at[1, pl.ds(EDGE, HALO), lanes]))
    start(loads)

    stages = []
    if finish is not None:
        stages += finish_plan(finish, last)
    if prepare is not None:
        stages += prepare_plan(prepare, last)
    slot = 0
    slots, waits = [], []
    for steps in stages:
        mine, copies = [], []
        for _, _, source, index in steps:
            if source == "own":
                y_source, w_source = y_ref.at[index], w_ref.at[index]
            else:
                ref = above_ref if source == "above" else below_ref
                height = (ref.shape[0] - 2 * HALO) // 2
                y_source = ref.at[pl.ds(2 * HALO + 64 * index, 64)]
                w_source = ref.at[pl.ds(2 * HALO + height + 64 * index, 64)]
            copies += [copy(y_source, y.at[slot]), copy(w_source, w.at[slot])]
            mine.append(slot)
            slot += 1
        start(copies)
        slots.append(mine)
        waits.append(copies)
    passing, sending = [], []
    if prepare is not None:
        for windows, out in zip(sent_reflectors(prepare, last), bundle_refs):
            at = 2 * HALO
            for index in windows:
                passing += [copy(y_ref.at[index], y.at[slot]), copy(w_ref.at[index], w.at[slot])]
                sending += [
                    copy(y.at[slot], out.at[pl.ds(at, 64)]),
                    copy(w.at[slot], out.at[pl.ds(at + 64 * len(windows), 64)]),
                ]
                slot += 1
                at += 64
    start(passing)
    wait(loads)

    def stage(number):
        wait(waits[number])
        blocks = [
            (side[which, pl.ds(row, 128), :], y[slots[number][j]], w[slots[number][j]])
            for j, (which, row, _, _) in enumerate(stages[number])
        ]
        for (which, row, _, _), value in zip(stages[number], band_steps(blocks)):
            side[which, pl.ds(row, 128), :] = value

    stores = []
    first = 0
    if finish is not None:
        first = 3
        for number in range(first):
            stage(number)
        out_ref[pl.ds(0, EDGE), :] = side[0, pl.ds(HALO, EDGE), :]
        out_ref[pl.ds(rows - EDGE, EDGE), :] = side[1, pl.ds(0, EDGE), :]
    wait(passing)
    start(sending)
    if prepare is not None:
        for number in range(first, first + 2):
            stage(number)
        for j in range(2):
            part, lanes = pl.ds(j * HALO, HALO), pl.ds(j * 128, 128)
            stores.append(copy(side.at[1, pl.ds(EDGE - HALO, HALO), lanes], bundle_refs[0].at[part]))
            stores.append(copy(side.at[0, pl.ds(HALO, HALO), lanes], bundle_refs[1].at[part]))
        start(stores)
    wait(stores + sending)


def edges(finish, prepare, x, y, w, halos=()):
    last = y.shape[1] - 1
    out_shape = []
    if finish is not None:
        out_shape.append(jax.ShapeDtypeStruct(x.shape, F32))
    if prepare is not None:
        out_shape += bundles(last)
    in_vmem = VMEM_SPEC if finish is not None else ANY
    return pl.pallas_call(
        functools.partial(edge_kernel, finish, prepare, last),
        out_shape=out_shape,
        in_specs=[in_vmem] + [ANY] * (2 + len(halos)),
        out_specs=[in_vmem] + [ANY] * (len(out_shape) - 1),
        scratch_shapes=[
            pltpu.VMEM((2, HALO + EDGE, x.shape[1]), F32),
            pltpu.VMEM((20,) + y.shape[2:], F32),
            pltpu.VMEM((20,) + w.shape[2:], F32),
            pltpu.SemaphoreType.DMA((80,)),
        ],
        input_output_aliases={} if finish is None else {0: 0},
        compiler_params=pltpu.CompilerParams(vmem_limit_bytes=EDGE_VMEM if finish is not None else 63 * MIB),
        cost_estimate=pl.CostEstimate(flops=1_500_000_000, bytes_accessed=3_000_000, transcendentals=0),
        name="edges",
    )(x, y, w, *halos)


def relay_kernel(left_ref, right_ref, own_ref, after_ref, trio_ref, low_ref, high_ref, trio, sem):
    height = left_ref.shape[0]
    half = height // 2
    left = pltpu.make_async_copy(left_ref, trio.at[pl.ds(height, height)], sem.at[0])
    right = pltpu.make_async_copy(right_ref, trio.at[pl.ds(2 * height, height)], sem.at[1])
    own = pltpu.make_async_copy(own_ref, trio.at[pl.ds(0, height)], sem.at[2])
    for copy in (left, right, own):
        copy.start()
    left.wait()
    low = pltpu.make_async_copy(trio.at[pl.ds(height, half)], low_ref, sem.at[3])
    low.start()
    right.wait()
    high = pltpu.make_async_copy(trio.at[pl.ds(2 * height + half, half)], high_ref, sem.at[4])
    high.start()
    own.wait()
    whole = pltpu.make_async_copy(trio, trio_ref, sem.at[5])
    whole.start()
    for copy in (low, high, whole):
        copy.wait()


def relay(left, right, own, after):
    height, rows = own.shape
    return pl.pallas_call(
        relay_kernel,
        out_shape=[jax.ShapeDtypeStruct((part, rows), F32) for part in (3 * height, height // 2, height // 2)],
        in_specs=[ANY] * 4,
        out_specs=[ANY] * 3,
        scratch_shapes=[pltpu.VMEM((3 * height, rows), F32), pltpu.SemaphoreType.DMA((6,))],
        compiler_params=pltpu.CompilerParams(vmem_limit_bytes=EDGE_VMEM),
        cost_estimate=pl.CostEstimate(flops=0, bytes_accessed=5_000_000, transcendentals=0),
        name="relay",
    )(left, right, own, after)


TILE = 256
BY_ROWS = (((1,), (1,)), ((), ()))


def spans(rows, number):
    tiles = rows // TILE
    cuts = [tiles * i // number * TILE for i in range(number + 1)]
    return [(start, stop - start) for start, stop in zip(cuts, cuts[1:])]


def stacked3(left, right, dims=(((1,), (0,)), ((), ()))):
    (left_high, left_low), (right_high, right_low) = left, right
    rows = left_high.shape[0]
    both = dot(jnp.concatenate([left_high, left_low], axis=0), right_high, dims)
    return both[:rows] + both[rows:] + dot(left_high, right_low, dims)


def panel_places(height):
    at_x, at_core = lax.axis_index("x"), lax.axis_index("core")
    places = []
    for parts in (((0, 0), (-1, 0), (1, 0)), ((2, 0),), ((2, height // 2),)):
        for twin in (0, 1):
            for shift, skip in parts:
                col = lax.rem(at_x + 4 + shift, 4) * 2 + lax.rem(at_core + twin, 2)
                places.append(col * height + skip)
    return places


def coeffs_kernel(shares, width, x_ref, t_ref, *refs):
    *pieces, out_ref, panel_ref, t, panel, t_sem, sem = refs
    total = x_ref.shape[0]
    half = width // 2
    t_load = pltpu.make_async_copy(t_ref, t, t_sem.at[0])
    t_load.start()
    parts = spans(x_ref.shape[0], 2)
    height = 2 * pieces[-1].shape[0]
    places = panel_places(height)
    loads = []
    for number, (start, length) in enumerate(parts):
        span = pl.ds(start, length)
        copies = []
        for piece in pieces:
            step = min(height, piece.shape[0])
            for at in range(0, piece.shape[0], step):
                rows = pl.ds(pl.multiple_of(places[len(copies)], step), step)
                copies.append(
                    pltpu.make_async_copy(
                        piece.at[pl.ds(at, step), span], panel.at[rows, span], sem.at[number, len(copies)]
                    )
                )
        loads.append(copies)
    for copies in loads:
        for copy in copies:
            copy.start()
    coeffs = gram = None
    stores = []
    t_load.wait()
    for i in range(2):
        beside = panel_ref.at[pl.ds(i * width, width), pl.ds(total, width)]
        stores.append(pltpu.make_async_copy(t.at[i], beside, t_sem.at[i]))
        stores[-1].start()
    for number, ((start, length), copies) in enumerate(zip(parts, loads)):
        for copy in copies:
            copy.wait()
        span = pl.ds(start, length)
        stores.append(pltpu.make_async_copy(panel.at[:, span], panel_ref.at[:, span], sem.at[number, 10]))
        stores[-1].start()
        span = slice(start, start + length)
        high, low = split(panel[:, span])
        part = stacked3((high, low), split(x_ref[span, :]))
        mine = split(panel[pl.ds(pl.multiple_of(lax.axis_index("core") * half, half), half), span])
        gram_part = stacked3((high[width:], low[width:]), mine, BY_ROWS)
        coeffs = part if coeffs is None else coeffs + part
        gram = gram_part if gram is None else gram + gram_part
    a = 2 * width // shares
    out_ref[:, :a, :] = coeffs[:, :half].reshape(shares, a, half)
    out_ref[:, a : 2 * a, :] = coeffs[:, half:].reshape(shares, a, half)
    out_ref[:, 2 * a :, :] = gram.reshape(shares, width // shares, half)
    for copy in stores:
        copy.wait()


def panel_coeffs(shares, x, t, pieces):
    width = t.shape[1]
    return pl.pallas_call(
        functools.partial(coeffs_kernel, shares, width),
        out_shape=[
            jax.ShapeDtypeStruct((shares, 5 * width // shares, width // 2), F32),
            jax.ShapeDtypeStruct((2 * width, x.shape[0] + width), F32),
        ],
        in_specs=[VMEM_SPEC] + [ANY] * (1 + len(pieces)),
        out_specs=[VMEM_SPEC, ANY],
        scratch_shapes=[
            pltpu.VMEM(t.shape, F32),
            pltpu.VMEM((2 * width, x.shape[0]), F32),
            pltpu.SemaphoreType.DMA((2,)),
            pltpu.SemaphoreType.DMA((2, 11)),
        ],
        compiler_params=pltpu.CompilerParams(vmem_limit_bytes=COEFFS_VMEM),
        cost_estimate=pl.CostEstimate(flops=4_000_000_000, bytes_accessed=11_000_000, transcendentals=0),
        name="panel_coeffs",
    )(x, t, *pieces)


def update_kernel(width, sums_ref, x_ref, panel_ref, twin_ref, out_ref, panel, stage, twin, t_sem, twin_sem, sem):
    rows = stage.shape[0]
    parts = spans(rows, 4)
    span = pl.ds(rows, width)
    t_load = pltpu.make_async_copy(panel_ref.at[:, span], panel.at[:, span], t_sem)
    t_load.start()
    a = 2 * width // sums_ref.shape[0]
    twin_load = pltpu.make_async_copy(twin_ref.at[:, pl.ds(2 * a, a // 2)], twin, twin_sem)
    twin_load.start()
    loads = []
    for number, (start, length) in enumerate(parts):
        span = pl.ds(start, length)
        loads.append(pltpu.make_async_copy(panel_ref.at[:, span], panel.at[:, span], sem.at[0, number]))
        loads[-1].start()
    half = width // 2
    whole = [sums_ref[:, i * a : (i + 1) * a, :].reshape(2 * width, half) for i in range(2)]
    coeffs = jnp.concatenate(whole, axis=1)
    t_load.wait()
    t = panel[:, rows:]
    first = dot3(split(t[:width]), split(coeffs[:width]))
    twin_load.wait()
    mine, other = sums_ref[:, 2 * a :, :].reshape(width, half), twin[...].reshape(width, half)
    is_first = lax.axis_index("core") == 0
    gram = jnp.concatenate([jnp.where(is_first, mine, other), jnp.where(is_first, other, mine)], axis=1)
    rest = coeffs[width:] - dot3(split(gram), split(first))
    second = dot3(split(t[width:]), split(rest))
    right = split(jnp.concatenate([first, second], axis=0))
    stores = []
    for number, (start, length) in enumerate(parts):
        loads[number].wait()
        for at in range(start, start + length, TILE):
            span = slice(at, at + TILE)
            high, low = split(panel[:, span])
            stage[span, :] = x_ref[span, :] - stacked3((high.T, low.T), right)
        span = pl.ds(start, length)
        stores.append(pltpu.make_async_copy(stage.at[span], out_ref.at[span], sem.at[1, number]))
        stores[-1].start()
    for copy in stores:
        copy.wait()


def update(sums, x, panel, twin, width):
    return pl.pallas_call(
        functools.partial(update_kernel, width),
        out_shape=jax.ShapeDtypeStruct(x.shape, F32),
        in_specs=[VMEM_SPEC, VMEM_SPEC, ANY, ANY],
        out_specs=ANY,
        scratch_shapes=[
            pltpu.VMEM(panel.shape, F32),
            pltpu.VMEM(x.shape, F32),
            pltpu.VMEM((sums.shape[0], width // sums.shape[0], width // 2), F32),
            pltpu.SemaphoreType.DMA,
            pltpu.SemaphoreType.DMA,
            pltpu.SemaphoreType.DMA((2, 4)),
        ],
        compiler_params=pltpu.CompilerParams(vmem_limit_bytes=UPDATE_VMEM),
        cost_estimate=pl.CostEstimate(flops=3_000_000_000, bytes_accessed=14_000_000, transcendentals=0),
        name="update",
    )(sums, x, panel, twin)


def send(value, axis, steps):
    count = lax.axis_size(axis)
    return lax.ppermute(value, axis, [(i, (i + steps) % count) for i in range(count)])


def per_device(eigvecs, reflect_y, reflect_w, panel_v, panel_t):
    rows = ("z", "y")
    shares = lax.axis_size(rows)
    own = panel_v.T

    from_left = send(own, "x", 1)
    from_right = send(own, "x", -1)
    for_below, for_above = edges(None, 0, eigvecs, reflect_y, reflect_w)
    above, below = send(for_below, rows, 1), send(for_above, rows, -1)

    x = interior(0, eigvecs, reflect_y, reflect_w)
    x, for_below, for_above = edges(0, 4, x, reflect_y, reflect_w, (above, below))
    trio, low, high = relay(from_left, from_right, own, for_below)
    low, high = send(low, "x", 1), send(high, "x", -1)
    above, below = send(for_below, rows, 1), send(for_above, rows, -1)
    twin_trio = send(trio, "core", 1)

    x = interior(4, x, reflect_y, reflect_w)
    x, low, high, above, below = lax.optimization_barrier((x, low, high, above, below))
    twin_low, twin_high = send(low, "core", 1), send(high, "core", 1)
    (x,) = edges(4, None, x, reflect_y, reflect_w, (above, below))

    pieces = [trio, twin_trio, low, twin_low, high, twin_high]
    sums, panel = panel_coeffs(shares, x, panel_t, pieces)
    mine = jnp.sum(lax.all_to_all(sums, rows, 0, 0), axis=0)
    sums = lax.all_to_all(jnp.broadcast_to(mine[None], sums.shape), rows, 0, 0)
    return update(sums, x, panel, send(sums, "core", 1), panel_t.shape[1])


def solution(mesh):
    z, y, x, core = 8, 4, 4, 2
    fine = Mesh(mesh.devices.reshape(z, y, x, core), ("z", "y", "x", "core"))
    row, col = ("z", "y"), ("x", "core")
    return jax.shard_map(
        per_device,
        mesh=fine,
        in_specs=(
            P(row, col),
            P(None, row, None, None),
            P(None, row, None, None),
            P(row, col),
            P(),
        ),
        out_specs=P(row, col),
        check_vma=False,
    )
```

```python
import functools

import jax
import jax.numpy as jnp
from jax import lax
from jax.experimental import pallas as pl
from jax.experimental.pallas import tpu as pltpu
from jax.sharding import Mesh, PartitionSpec as P

HALO = 128
EDGE = 256
PARTS = 3
GROUP = 9
ANY = pl.BlockSpec(memory_space=pl.ANY)
VMEM_SPEC = pl.BlockSpec(memory_space=pltpu.VMEM)
F32 = jnp.float32
BF16 = jnp.bfloat16
MIB = 1024 * 1024
INTERIOR_VMEM = 48 * MIB
EDGE_VMEM = 44 * MIB
COEFFS_VMEM = 40 * MIB
UPDATE_VMEM = 44 * MIB


def split(value):
    high = value.astype(BF16)
    low = (value - high.astype(F32)).astype(BF16)
    return high, low


def dot(left, right, dims=(((1,), (0,)), ((), ()))):
    return lax.dot_general(left, right, dims, preferred_element_type=F32)


def dot3(left, right, dims=(((1,), (0,)), ((), ()))):
    left_high, left_low = left
    right_high, right_low = right
    return (
        dot(left_high, right_low, dims) + dot(left_low, right_high, dims) + dot(left_high, right_high, dims)
    )


def band_steps(blocks):
    projected = []
    for z, y, _ in blocks:
        z_high, z_low = split(z)
        y_high, y_low = split(y)
        left = jnp.concatenate(
            [jnp.concatenate([y_high, y_high], axis=1), jnp.concatenate([y_low, y_low], axis=1)], axis=0
        )
        both = dot(left, jnp.concatenate([z_high, z_low], axis=0))
        half = y.shape[0]
        projected.append(both[:half] + both[half:])
    out = []
    for (z, _, w), p in zip(blocks, projected):
        p_high, p_low = split(p)
        w_high, w_low = split(w)
        turned = jnp.concatenate([w_high, w_low], axis=0).T
        left = jnp.concatenate([turned, turned], axis=1)
        out.append(z - dot(left, jnp.concatenate([p_high, p_high, p_low, p_low], axis=0)))
    return out


def interior_kernel(base, x_ref, y_ref, w_ref, x, y, w, first_sem, sweep_sem):
    windows = y.shape[1]
    cuts = [windows * part // PARTS for part in range(PARTS + 1)]
    first, later = [], []
    for part in range(PARTS):
        start, number = cuts[part], cuts[part + 1] - cuts[part]
        span = pl.ds(start * 128, number * 128)
        some = pl.ds(start, number)
        copies = [
            pltpu.make_async_copy(y_ref.at[base, some], y.at[0, some], first_sem.at[1, part]),
            pltpu.make_async_copy(w_ref.at[base, some], w.at[0, some], first_sem.at[2, part]),
        ]
        if base == 0:
            copies.append(pltpu.make_async_copy(x_ref.at[span], x.at[span], first_sem.at[0, part]))
        first.append(copies)
    for s in range(1, 4):
        later.append(
            (
                pltpu.make_async_copy(y_ref.at[base + s], y.at[s], sweep_sem.at[0, s]),
                pltpu.make_async_copy(w_ref.at[base + s], w.at[s], sweep_sem.at[1, s]),
            )
        )
    for copies in first + later:
        for copy in copies:
            copy.start()

    def run(s, start, stop):
        rows_of = [pl.ds(v * 128 + 64 * (s % 2), 128) for v in range(start, stop)]
        blocks = [(x[at, :], y[s, v], w[s, v]) for at, v in zip(rows_of, range(start, stop))]
        for at, value in zip(rows_of, band_steps(blocks)):
            x[at, :] = value

    for part in range(PARTS):
        for copy in first[part]:
            copy.wait()
        run(0, cuts[part], cuts[part + 1])
    for s in range(1, 4):
        for copy in later[s - 1]:
            copy.wait()
        begin, end = s // 2, s // 2 + windows - s
        for start in range(begin, end, GROUP):
            run(s, start, min(start + GROUP, end))


def interior(base, x, y, w):
    return pl.pallas_call(
        functools.partial(interior_kernel, base),
        out_shape=jax.ShapeDtypeStruct(x.shape, F32),
        in_specs=[VMEM_SPEC if base else ANY, ANY, ANY],
        out_specs=VMEM_SPEC,
        scratch_shapes=[
            pltpu.VMEM((4,) + y.shape[1:], F32),
            pltpu.VMEM((4,) + w.shape[1:], F32),
            pltpu.SemaphoreType.DMA((3, PARTS)),
            pltpu.SemaphoreType.DMA((2, 4)),
        ],
        input_output_aliases={0: 0} if base else {},
        compiler_params=pltpu.CompilerParams(vmem_limit_bytes=INTERIOR_VMEM),
        cost_estimate=pl.CostEstimate(flops=2_000_000_000, bytes_accessed=1_000_000, transcendentals=0),
        name=f"interior{base}",
    )(x, y, w)


def prepare_plan(base, last):
    return [
        [
            (0, 128, "own", (base, 0)),
            (0, 256, "own", (base, 1)),
            (1, 0, "own", (base, last - 1)),
            (1, 128, "own", (base, last)),
        ],
        [(0, 192, "own", (base + 1, 0)), (1, 64, "own", (base + 1, last - 1))],
    ]


def finish_plan(base, last):
    return [
        [(0, 64, "above", 0), (1, 192, "own", (base + 1, last))],
        [
            (0, 0, "above", 1),
            (0, 128, "own", (base + 2, 0)),
            (1, 128, "own", (base + 2, last)),
            (1, 256, "below", 0),
        ],
        [
            (0, 64, "above", 2),
            (0, 192, "own", (base + 3, 0)),
            (1, 64, "own", (base + 3, last - 1)),
            (1, 192, "own", (base + 3, last)),
        ],
    ]


def sent_reflectors(base, last):
    return [(base + 1, last), (base + 2, last), (base + 3, last)], [(base + 2, 0)]


def bundles(last):
    return [
        jax.ShapeDtypeStruct((2 * HALO + 2 * 64 * len(windows), 128), F32) for windows in sent_reflectors(0, last)
    ]


def edge_kernel(finish, prepare, last, *refs):
    refs = list(refs)
    take = lambda number: [refs.pop(0) for _ in range(number)]
    x_ref, y_ref, w_ref = take(3)
    above_ref = below_ref = None
    if finish is not None:
        above_ref, below_ref = take(2)
    if finish is not None:
        (out_ref,) = take(1)
    if prepare is not None:
        bundle_refs = take(2)
    side, y, w, sem = refs
    rows = x_ref.shape[0]
    used = [0]

    def copy(source, target):
        used[0] += 1
        return pltpu.make_async_copy(source, target, sem.at[used[0] - 1])

    def start(copies):
        for one in copies:
            one.start()

    def wait(copies):
        for one in copies:
            one.wait()

    loads = []
    if finish is None:
        loads = [
            copy(x_ref.at[pl.ds(0, EDGE)], side.at[0, pl.ds(HALO, EDGE)]),
            copy(x_ref.at[pl.ds(rows - EDGE, EDGE)], side.at[1, pl.ds(0, EDGE)]),
        ]
    else:
        side[0, pl.ds(HALO, EDGE), :] = x_ref[pl.ds(0, EDGE), :]
        side[1, pl.ds(0, EDGE), :] = x_ref[pl.ds(rows - EDGE, EDGE), :]
        for j in range(2):
            part, lanes = pl.ds(j * HALO, HALO), pl.ds(j * 128, 128)
            loads.append(copy(above_ref.at[part], side.at[0, pl.ds(0, HALO), lanes]))
            loads.append(copy(below_ref.at[part], side.at[1, pl.ds(EDGE, HALO), lanes]))
    start(loads)

    stages = []
    if finish is not None:
        stages += finish_plan(finish, last)
    if prepare is not None:
        stages += prepare_plan(prepare, last)
    slot = 0
    slots, waits = [], []
    for steps in stages:
        mine, copies = [], []
        for _, _, source, index in steps:
            if source == "own":
                y_source, w_source = y_ref.at[index], w_ref.at[index]
            else:
                ref = above_ref if source == "above" else below_ref
                height = (ref.shape[0] - 2 * HALO) // 2
                y_source = ref.at[pl.ds(2 * HALO + 64 * index, 64)]
                w_source = ref.at[pl.ds(2 * HALO + height + 64 * index, 64)]
            copies += [copy(y_source, y.at[slot]), copy(w_source, w.at[slot])]
            mine.append(slot)
            slot += 1
        start(copies)
        slots.append(mine)
        waits.append(copies)
    passing, sending = [], []
    if prepare is not None:
        for windows, out in zip(sent_reflectors(prepare, last), bundle_refs):
            at = 2 * HALO
            for index in windows:
                passing += [copy(y_ref.at[index], y.at[slot]), copy(w_ref.at[index], w.at[slot])]
                sending += [
                    copy(y.at[slot], out.at[pl.ds(at, 64)]),
                    copy(w.at[slot], out.at[pl.ds(at + 64 * len(windows), 64)]),
                ]
                slot += 1
                at += 64
    start(passing)
    wait(loads)

    def stage(number):
        wait(waits[number])
        blocks = [
            (side[which, pl.ds(row, 128), :], y[slots[number][j]], w[slots[number][j]])
            for j, (which, row, _, _) in enumerate(stages[number])
        ]
        for (which, row, _, _), value in zip(stages[number], band_steps(blocks)):
            side[which, pl.ds(row, 128), :] = value

    stores = []
    first = 0
    if finish is not None:
        first = 3
        for number in range(first):
            stage(number)
        out_ref[pl.ds(0, EDGE), :] = side[0, pl.ds(HALO, EDGE), :]
        out_ref[pl.ds(rows - EDGE, EDGE), :] = side[1, pl.ds(0, EDGE), :]
    wait(passing)
    start(sending)
    if prepare is not None:
        for number in range(first, first + 2):
            stage(number)
        for j in range(2):
            part, lanes = pl.ds(j * HALO, HALO), pl.ds(j * 128, 128)
            stores.append(copy(side.at[1, pl.ds(EDGE - HALO, HALO), lanes], bundle_refs[0].at[part]))
            stores.append(copy(side.at[0, pl.ds(HALO, HALO), lanes], bundle_refs[1].at[part]))
        start(stores)
    wait(stores + sending)


def edges(finish, prepare, x, y, w, halos=()):
    last = y.shape[1] - 1
    out_shape = []
    if finish is not None:
        out_shape.append(jax.ShapeDtypeStruct(x.shape, F32))
    if prepare is not None:
        out_shape += bundles(last)
    in_vmem = VMEM_SPEC if finish is not None else ANY
    return pl.pallas_call(
        functools.partial(edge_kernel, finish, prepare, last),
        out_shape=out_shape,
        in_specs=[in_vmem] + [ANY] * (2 + len(halos)),
        out_specs=[in_vmem] + [ANY] * (len(out_shape) - 1),
        scratch_shapes=[
            pltpu.VMEM((2, HALO + EDGE, x.shape[1]), F32),
            pltpu.VMEM((20,) + y.shape[2:], F32),
            pltpu.VMEM((20,) + w.shape[2:], F32),
            pltpu.SemaphoreType.DMA((80,)),
        ],
        input_output_aliases={} if finish is None else {0: 0},
        compiler_params=pltpu.CompilerParams(vmem_limit_bytes=EDGE_VMEM if finish is not None else 63 * MIB),
        cost_estimate=pl.CostEstimate(flops=1_500_000_000, bytes_accessed=3_000_000, transcendentals=0),
        name="edges",
    )(x, y, w, *halos)


def relay_kernel(left_ref, right_ref, own_ref, after_ref, trio_ref, low_ref, high_ref, trio, sem):
    height = left_ref.shape[0]
    half = height // 2
    left = pltpu.make_async_copy(left_ref, trio.at[pl.ds(height, height)], sem.at[0])
    right = pltpu.make_async_copy(right_ref, trio.at[pl.ds(2 * height, height)], sem.at[1])
    own = pltpu.make_async_copy(own_ref, trio.at[pl.ds(0, height)], sem.at[2])
    for copy in (left, right, own):
        copy.start()
    left.wait()
    low = pltpu.make_async_copy(trio.at[pl.ds(height, half)], low_ref, sem.at[3])
    low.start()
    right.wait()
    high = pltpu.make_async_copy(trio.at[pl.ds(2 * height + half, half)], high_ref, sem.at[4])
    high.start()
    own.wait()
    whole = pltpu.make_async_copy(trio, trio_ref, sem.at[5])
    whole.start()
    for copy in (low, high, whole):
        copy.wait()


def relay(left, right, own, after):
    height, rows = own.shape
    return pl.pallas_call(
        relay_kernel,
        out_shape=[jax.ShapeDtypeStruct((part, rows), F32) for part in (3 * height, height // 2, height // 2)],
        in_specs=[ANY] * 4,
        out_specs=[ANY] * 3,
        scratch_shapes=[pltpu.VMEM((3 * height, rows), F32), pltpu.SemaphoreType.DMA((6,))],
        compiler_params=pltpu.CompilerParams(vmem_limit_bytes=EDGE_VMEM),
        cost_estimate=pl.CostEstimate(flops=0, bytes_accessed=5_000_000, transcendentals=0),
        name="relay",
    )(left, right, own, after)


TILE = 256
COEFFS_PARTS = (0, 1)
UPDATE_PARTS = (0, 0.5, 1)
BY_ROWS = (((1,), (1,)), ((), ()))


def spans(rows, parts):
    tiles = rows // TILE
    cuts = [round(tiles * part) * TILE for part in parts]
    return [(start, stop - start) for start, stop in zip(cuts, cuts[1:])]


def stacked3(left, right, dims=(((1,), (0,)), ((), ()))):
    (left_high, left_low), (right_high, right_low) = left, right
    rows = left_high.shape[0]
    both = dot(jnp.concatenate([left_high, left_low], axis=0), right_high, dims)
    return both[:rows] + both[rows:] + dot(left_high, right_low, dims)


def panel_places(height):
    at_x, at_core = lax.axis_index("x"), lax.axis_index("core")
    places = []
    for parts in (((0, 0), (-1, 0), (1, 0)), ((2, 0),), ((2, height // 2),)):
        for twin in (0, 1):
            for shift, skip in parts:
                col = lax.rem(at_x + 4 + shift, 4) * 2 + lax.rem(at_core + twin, 2)
                places.append(col * height + skip)
    return places


def coeffs_kernel(shares, width, x_ref, t_ref, *refs):
    *pieces, out_ref, panel_ref, t, panel, t_sem, sem = refs
    total = x_ref.shape[0]
    half = width // 2
    t_load = pltpu.make_async_copy(t_ref, t, t_sem.at[0])
    t_load.start()
    parts = spans(x_ref.shape[0], COEFFS_PARTS)
    height = 2 * pieces[-1].shape[0]
    places = panel_places(height)
    loads = []
    for number, (start, length) in enumerate(parts):
        span = pl.ds(start, length)
        copies = []
        for piece in pieces:
            step = min(height, piece.shape[0])
            for at in range(0, piece.shape[0], step):
                rows = pl.ds(pl.multiple_of(places[len(copies)], step), step)
                copies.append(
                    pltpu.make_async_copy(
                        piece.at[pl.ds(at, step), span], panel.at[rows, span], sem.at[number, len(copies)]
                    )
                )
        loads.append(copies)
    for copies in loads:
        for copy in copies:
            copy.start()
    coeffs = gram = None
    stores = []
    t_load.wait()
    for i in range(2):
        beside = panel_ref.at[pl.ds(i * width, width), pl.ds(total, width)]
        stores.append(pltpu.make_async_copy(t.at[i], beside, t_sem.at[i]))
        stores[-1].start()
    for number, ((start, length), copies) in enumerate(zip(parts, loads)):
        for copy in copies:
            copy.wait()
        span = pl.ds(start, length)
        stores.append(pltpu.make_async_copy(panel.at[:, span], panel_ref.at[:, span], sem.at[number, 10]))
        stores[-1].start()
        span = slice(start, start + length)
        high, low = split(panel[:, span])
        part = stacked3((high, low), split(x_ref[span, :]))
        mine = split(panel[pl.ds(pl.multiple_of(lax.axis_index("core") * half, half), half), span])
        gram_part = stacked3((high[width:], low[width:]), mine, BY_ROWS)
        coeffs = part if coeffs is None else coeffs + part
        gram = gram_part if gram is None else gram + gram_part
    a = 2 * width // shares
    out_ref[:, :a, :] = coeffs[:, :half].reshape(shares, a, half)
    out_ref[:, a : 2 * a, :] = coeffs[:, half:].reshape(shares, a, half)
    out_ref[:, 2 * a :, :] = gram.reshape(shares, width // shares, half)
    for copy in stores:
        copy.wait()


def panel_coeffs(shares, x, t, pieces):
    width = t.shape[1]
    return pl.pallas_call(
        functools.partial(coeffs_kernel, shares, width),
        out_shape=[
            jax.ShapeDtypeStruct((shares, 5 * width // shares, width // 2), F32),
            jax.ShapeDtypeStruct((2 * width, x.shape[0] + width), F32),
        ],
        in_specs=[VMEM_SPEC] + [ANY] * (1 + len(pieces)),
        out_specs=[VMEM_SPEC, ANY],
        scratch_shapes=[
            pltpu.VMEM(t.shape, F32),
            pltpu.VMEM((2 * width, x.shape[0]), F32),
            pltpu.SemaphoreType.DMA((2,)),
            pltpu.SemaphoreType.DMA((len(COEFFS_PARTS) - 1, 11)),
        ],
        compiler_params=pltpu.CompilerParams(vmem_limit_bytes=COEFFS_VMEM),
        cost_estimate=pl.CostEstimate(flops=4_000_000_000, bytes_accessed=11_000_000, transcendentals=0),
        name="panel_coeffs",
    )(x, t, *pieces)


def update_kernel(width, sums_ref, x_ref, panel_ref, twin_ref, out_ref, panel, stage, twin, t_sem, twin_sem, sem):
    rows = stage.shape[0]
    parts = spans(rows, UPDATE_PARTS)
    span = pl.ds(rows, width)
    t_load = pltpu.make_async_copy(panel_ref.at[:, span], panel.at[:, span], t_sem)
    t_load.start()
    a = 2 * width // sums_ref.shape[0]
    twin_load = pltpu.make_async_copy(twin_ref.at[:, pl.ds(2 * a, a // 2)], twin, twin_sem)
    twin_load.start()
    loads = []
    for number, (start, length) in enumerate(parts):
        span = pl.ds(start, length)
        loads.append(pltpu.make_async_copy(panel_ref.at[:, span], panel.at[:, span], sem.at[0, number]))
        loads[-1].start()
    half = width // 2
    whole = [sums_ref[:, i * a : (i + 1) * a, :].reshape(2 * width, half) for i in range(2)]
    coeffs = jnp.concatenate(whole, axis=1)
    t_load.wait()
    t = panel[:, rows:]
    first = dot3(split(t[:width]), split(coeffs[:width]))
    twin_load.wait()
    mine, other = sums_ref[:, 2 * a :, :].reshape(width, half), twin[...].reshape(width, half)
    is_first = lax.axis_index("core") == 0
    gram = jnp.concatenate([jnp.where(is_first, mine, other), jnp.where(is_first, other, mine)], axis=1)
    rest = coeffs[width:] - dot3(split(gram), split(first))
    second = dot3(split(t[width:]), split(rest))
    right = split(jnp.concatenate([first, second], axis=0))
    stores = []
    for number, (start, length) in enumerate(parts):
        loads[number].wait()
        for at in range(start, start + length, TILE):
            span = slice(at, at + TILE)
            high, low = split(panel[:, span])
            stage[span, :] = x_ref[span, :] - stacked3((high.T, low.T), right)
        span = pl.ds(start, length)
        stores.append(pltpu.make_async_copy(stage.at[span], out_ref.at[span], sem.at[1, number]))
        stores[-1].start()
    for copy in stores:
        copy.wait()


def update(sums, x, panel, twin, width):
    return pl.pallas_call(
        functools.partial(update_kernel, width),
        out_shape=jax.ShapeDtypeStruct(x.shape, F32),
        in_specs=[VMEM_SPEC, VMEM_SPEC, ANY, ANY],
        out_specs=ANY,
        scratch_shapes=[
            pltpu.VMEM(panel.shape, F32),
            pltpu.VMEM(x.shape, F32),
            pltpu.VMEM((sums.shape[0], width // sums.shape[0], width // 2), F32),
            pltpu.SemaphoreType.DMA,
            pltpu.SemaphoreType.DMA,
            pltpu.SemaphoreType.DMA((2, len(UPDATE_PARTS) - 1)),
        ],
        compiler_params=pltpu.CompilerParams(vmem_limit_bytes=UPDATE_VMEM),
        cost_estimate=pl.CostEstimate(flops=3_000_000_000, bytes_accessed=14_000_000, transcendentals=0),
        name="update",
    )(sums, x, panel, twin)


def send(value, axis, steps):
    count = lax.axis_size(axis)
    return lax.ppermute(value, axis, [(i, (i + steps) % count) for i in range(count)])


def per_device(eigvecs, reflect_y, reflect_w, panel_v, panel_t):
    rows = ("z", "y")
    shares = lax.axis_size(rows)
    own = panel_v.T

    from_left = send(own, "x", 1)
    from_right = send(own, "x", -1)
    for_below, for_above = edges(None, 0, eigvecs, reflect_y, reflect_w)
    above, below = send(for_below, rows, 1), send(for_above, rows, -1)

    x = interior(0, eigvecs, reflect_y, reflect_w)
    x, for_below, for_above = edges(0, 4, x, reflect_y, reflect_w, (above, below))
    trio, low, high = relay(from_left, from_right, own, for_below)
    low, high = send(low, "x", 1), send(high, "x", -1)
    above, below = send(for_below, rows, 1), send(for_above, rows, -1)
    twin_trio = send(trio, "core", 1)

    x = interior(4, x, reflect_y, reflect_w)
    x, low, high, above, below = lax.optimization_barrier((x, low, high, above, below))
    twin_low, twin_high = send(low, "core", 1), send(high, "core", 1)
    (x,) = edges(4, None, x, reflect_y, reflect_w, (above, below))

    pieces = [trio, twin_trio, low, twin_low, high, twin_high]
    sums, panel = panel_coeffs(shares, x, panel_t, pieces)
    mine = jnp.sum(lax.all_to_all(sums, rows, 0, 0), axis=0)
    sums = lax.all_to_all(jnp.broadcast_to(mine[None], sums.shape), rows, 0, 0)
    return update(sums, x, panel, send(sums, "core", 1), panel_t.shape[1])


def solution(mesh):
    z, y, x, core = 8, 4, 4, 2
    fine = Mesh(mesh.devices.reshape(z, y, x, core), ("z", "y", "x", "core"))
    row, col = ("z", "y"), ("x", "core")
    return jax.shard_map(
        per_device,
        mesh=fine,
        in_specs=(
            P(row, col),
            P(None, row, None, None),
            P(None, row, None, None),
            P(row, col),
            P(),
        ),
        out_specs=P(row, col),
        check_vma=False,
    )
```

```python
import functools

import jax
import jax.numpy as jnp
from jax import lax
from jax.experimental import pallas as pl
from jax.experimental.pallas import tpu as pltpu
from jax.sharding import Mesh, PartitionSpec as P

HALO = 128
EDGE = 256
PARTS = 3
GROUP = 9
ANY = pl.BlockSpec(memory_space=pl.ANY)
VMEM_SPEC = pl.BlockSpec(memory_space=pltpu.VMEM)
F32 = jnp.float32
BF16 = jnp.bfloat16
MIB = 1024 * 1024
INTERIOR_VMEM = 48 * MIB
EDGE_VMEM = 44 * MIB
COEFFS_VMEM = 40 * MIB
UPDATE_VMEM = 44 * MIB


def split(value):
    high = value.astype(BF16)
    low = (value - high.astype(F32)).astype(BF16)
    return high, low


def dot(left, right, dims=(((1,), (0,)), ((), ()))):
    return lax.dot_general(left, right, dims, preferred_element_type=F32)


def dot3(left, right, dims=(((1,), (0,)), ((), ()))):
    left_high, left_low = left
    right_high, right_low = right
    return (
        dot(left_high, right_low, dims) + dot(left_low, right_high, dims) + dot(left_high, right_high, dims)
    )


def band_steps(blocks):
    projected = []
    for z, y, _ in blocks:
        z_high, z_low = split(z)
        y_high, y_low = split(y)
        left = jnp.concatenate(
            [jnp.concatenate([y_high, y_high], axis=1), jnp.concatenate([y_low, y_low], axis=1)], axis=0
        )
        both = dot(left, jnp.concatenate([z_high, z_low], axis=0))
        half = y.shape[0]
        projected.append(both[:half] + both[half:])
    out = []
    for (z, _, w), p in zip(blocks, projected):
        p_high, p_low = split(p)
        w_high, w_low = split(w)
        turned = jnp.concatenate([w_high, w_low], axis=0).T
        left = jnp.concatenate([turned, turned], axis=1)
        out.append(z - dot(left, jnp.concatenate([p_high, p_high, p_low, p_low], axis=0)))
    return out


def interior_kernel(base, x_ref, y_ref, w_ref, x, y, w, first_sem, sweep_sem):
    windows = y.shape[1]
    cuts = [windows * part // PARTS for part in range(PARTS + 1)]
    first, later = [], []
    for part in range(PARTS):
        start, number = cuts[part], cuts[part + 1] - cuts[part]
        span = pl.ds(start * 128, number * 128)
        some = pl.ds(start, number)
        copies = [
            pltpu.make_async_copy(y_ref.at[base, some], y.at[0, some], first_sem.at[1, part]),
            pltpu.make_async_copy(w_ref.at[base, some], w.at[0, some], first_sem.at[2, part]),
        ]
        if base == 0:
            copies.append(pltpu.make_async_copy(x_ref.at[span], x.at[span], first_sem.at[0, part]))
        first.append(copies)
    for s in range(1, 4):
        later.append(
            (
                pltpu.make_async_copy(y_ref.at[base + s], y.at[s], sweep_sem.at[0, s]),
                pltpu.make_async_copy(w_ref.at[base + s], w.at[s], sweep_sem.at[1, s]),
            )
        )
    for copies in first + later:
        for copy in copies:
            copy.start()

    def run(s, start, stop):
        rows_of = [pl.ds(v * 128 + 64 * (s % 2), 128) for v in range(start, stop)]
        blocks = [(x[at, :], y[s, v], w[s, v]) for at, v in zip(rows_of, range(start, stop))]
        for at, value in zip(rows_of, band_steps(blocks)):
            x[at, :] = value

    for part in range(PARTS):
        for copy in first[part]:
            copy.wait()
        run(0, cuts[part], cuts[part + 1])
    for s in range(1, 4):
        for copy in later[s - 1]:
            copy.wait()
        begin, end = s // 2, s // 2 + windows - s
        for start in range(begin, end, GROUP):
            run(s, start, min(start + GROUP, end))


def interior(base, x, y, w):
    return pl.pallas_call(
        functools.partial(interior_kernel, base),
        out_shape=jax.ShapeDtypeStruct(x.shape, F32),
        in_specs=[VMEM_SPEC if base else ANY, ANY, ANY],
        out_specs=VMEM_SPEC,
        scratch_shapes=[
            pltpu.VMEM((4,) + y.shape[1:], F32),
            pltpu.VMEM((4,) + w.shape[1:], F32),
            pltpu.SemaphoreType.DMA((3, PARTS)),
            pltpu.SemaphoreType.DMA((2, 4)),
        ],
        input_output_aliases={0: 0} if base else {},
        compiler_params=pltpu.CompilerParams(vmem_limit_bytes=INTERIOR_VMEM),
        cost_estimate=pl.CostEstimate(flops=2_000_000_000, bytes_accessed=1_000_000, transcendentals=0),
        name=f"interior{base}",
    )(x, y, w)


def prepare_plan(base, last):
    return [
        [
            (0, 128, "own", (base, 0)),
            (0, 256, "own", (base, 1)),
            (1, 0, "own", (base, last - 1)),
            (1, 128, "own", (base, last)),
        ],
        [(0, 192, "own", (base + 1, 0)), (1, 64, "own", (base + 1, last - 1))],
    ]


def finish_plan(base, last):
    return [
        [(0, 64, "above", 0), (1, 192, "own", (base + 1, last))],
        [
            (0, 0, "above", 1),
            (0, 128, "own", (base + 2, 0)),
            (1, 128, "own", (base + 2, last)),
            (1, 256, "below", 0),
        ],
        [
            (0, 64, "above", 2),
            (0, 192, "own", (base + 3, 0)),
            (1, 64, "own", (base + 3, last - 1)),
            (1, 192, "own", (base + 3, last)),
        ],
    ]


def sent_reflectors(base, last):
    return [(base + 1, last), (base + 2, last), (base + 3, last)], [(base + 2, 0)]


def bundles(last):
    return [
        jax.ShapeDtypeStruct((2 * HALO + 2 * 64 * len(windows), 128), F32) for windows in sent_reflectors(0, last)
    ]


def edge_kernel(finish, prepare, last, *refs):
    refs = list(refs)
    take = lambda number: [refs.pop(0) for _ in range(number)]
    x_ref, y_ref, w_ref = take(3)
    above_ref = below_ref = None
    if finish is not None:
        above_ref, below_ref = take(2)
    if finish is not None:
        (out_ref,) = take(1)
    if prepare is not None:
        bundle_refs = take(2)
    side, above, below, end, begin, first_box, last_box, sent_below, sent_above, sem = refs
    rows = x_ref.shape[0]
    used = [0]

    def copy(source, target):
        used[0] += 1
        return pltpu.make_async_copy(source, target, sem.at[used[0] - 1])

    def start(copies):
        for one in copies:
            one.start()

    def wait(copies):
        for one in copies:
            one.wait()

    loads = []
    if finish is None:
        loads = [
            copy(x_ref.at[pl.ds(0, EDGE)], side.at[0, pl.ds(HALO, EDGE)]),
            copy(x_ref.at[pl.ds(rows - EDGE, EDGE)], side.at[1, pl.ds(0, EDGE)]),
        ]
    else:
        side[0, pl.ds(HALO, EDGE), :] = x_ref[pl.ds(0, EDGE), :]
        side[1, pl.ds(0, EDGE), :] = x_ref[pl.ds(rows - EDGE, EDGE), :]
        for j in range(2):
            part, lanes = pl.ds(j * HALO, HALO), pl.ds(j * 128, 128)
            loads.append(copy(above_ref.at[part], side.at[0, pl.ds(0, HALO), lanes]))
            loads.append(copy(below_ref.at[part], side.at[1, pl.ds(EDGE, HALO), lanes]))
    start(loads)

    boxes = {}
    copies = []

    def load(key, target, *parts):
        boxes[key] = target
        for kind, source in enumerate(parts):
            copies.append(copy(source, target.at[kind]))

    if finish is not None:
        for key, ref, target in (("above", above_ref, above), ("below", below_ref, below)):
            height = (ref.shape[0] - 2 * HALO) // 2
            load(key, target, *[ref.at[pl.ds(2 * HALO + i * height, height)] for i in range(2)])
        later = pl.ds(finish + 1, 3)
        load("end", end, *[ref.at[later, pl.ds(last - 1, 2)] for ref in (y_ref, w_ref)])
        load("begin", begin, *[ref.at[pl.ds(finish + 2, 2), 0] for ref in (y_ref, w_ref)])
    start(copies)
    finish_waits, copies = copies, []
    if prepare is not None:
        sweeps = pl.ds(prepare, 2)
        load("first", first_box, *[ref.at[sweeps, pl.ds(0, 2)] for ref in (y_ref, w_ref)])
        load("last", last_box, *[ref.at[sweeps, pl.ds(last - 1, 2)] for ref in (y_ref, w_ref)])
    start(copies)
    prepare_waits = copies

    def reflectors(kind, source, index):
        if source != "own":
            return boxes[source][kind, pl.ds(64 * index, 64), :]
        sweep, window = index
        if prepare is not None and sweep >= prepare:
            if window < 2:
                return boxes["first"][kind, sweep - prepare, window]
            return boxes["last"][kind, sweep - prepare, window - last + 1]
        if window == 0:
            return boxes["begin"][kind, sweep - finish - 2]
        return boxes["end"][kind, sweep - finish - 1, window - last + 1]

    stages = []
    if finish is not None:
        stages += finish_plan(finish, last)
    if prepare is not None:
        stages += prepare_plan(prepare, last)
    passing, sending = [], []
    if prepare is not None:
        for windows, out, held in zip(sent_reflectors(prepare, last), bundle_refs, (sent_below, sent_above)):
            height = 64 * len(windows)
            for kind, ref in enumerate((y_ref, w_ref)):
                for i, index in enumerate(windows):
                    passing.append(copy(ref.at[index], held.at[kind, pl.ds(64 * i, 64)]))
                sending.append(copy(held.at[kind], out.at[pl.ds(2 * HALO + kind * height, height)]))
    start(passing)
    wait(loads)

    def stage(number):
        blocks = [
            (side[which, pl.ds(row, 128), :], reflectors(0, *source), reflectors(1, *source))
            for which, row, *source in stages[number]
        ]
        for (which, row, _, _), value in zip(stages[number], band_steps(blocks)):
            side[which, pl.ds(row, 128), :] = value

    stores = []
    first = 0
    if finish is not None:
        first = 3
        wait(finish_waits)
        for number in range(first):
            stage(number)
        out_ref[pl.ds(0, EDGE), :] = side[0, pl.ds(HALO, EDGE), :]
        out_ref[pl.ds(rows - EDGE, EDGE), :] = side[1, pl.ds(0, EDGE), :]
    wait(passing)
    start(sending)
    if prepare is not None:
        wait(prepare_waits)
        for number in range(first, first + 2):
            stage(number)
        for j in range(2):
            part, lanes = pl.ds(j * HALO, HALO), pl.ds(j * 128, 128)
            stores.append(copy(side.at[1, pl.ds(EDGE - HALO, HALO), lanes], bundle_refs[0].at[part]))
            stores.append(copy(side.at[0, pl.ds(HALO, HALO), lanes], bundle_refs[1].at[part]))
        start(stores)
    wait(stores + sending)


def edges(finish, prepare, x, y, w, halos=()):
    last = y.shape[1] - 1
    out_shape = []
    if finish is not None:
        out_shape.append(jax.ShapeDtypeStruct(x.shape, F32))
    if prepare is not None:
        out_shape += bundles(last)
    in_vmem = VMEM_SPEC if finish is not None else ANY
    return pl.pallas_call(
        functools.partial(edge_kernel, finish, prepare, last),
        out_shape=out_shape,
        in_specs=[in_vmem] + [ANY] * (2 + len(halos)),
        out_specs=[in_vmem] + [ANY] * (len(out_shape) - 1),
        scratch_shapes=[
            pltpu.VMEM((2, HALO + EDGE, x.shape[1]), F32),
            pltpu.VMEM((2, 192, 128), F32),
            pltpu.VMEM((2, 64, 128), F32),
            pltpu.VMEM((2, 3, 2) + y.shape[2:], F32),
            pltpu.VMEM((2, 2) + y.shape[2:], F32),
            pltpu.VMEM((2, 2, 2) + y.shape[2:], F32),
            pltpu.VMEM((2, 2, 2) + y.shape[2:], F32),
            pltpu.VMEM((2, 192, 128), F32),
            pltpu.VMEM((2, 64, 128), F32),
            pltpu.SemaphoreType.DMA((48,)),
        ],
        input_output_aliases={} if finish is None else {0: 0},
        compiler_params=pltpu.CompilerParams(vmem_limit_bytes=EDGE_VMEM if finish is not None else 63 * MIB),
        cost_estimate=pl.CostEstimate(flops=1_500_000_000, bytes_accessed=3_000_000, transcendentals=0),
        name="edges",
    )(x, y, w, *halos)


def relay_kernel(left_ref, right_ref, own_ref, after_ref, trio_ref, low_ref, high_ref, trio, sem):
    height = left_ref.shape[0]
    half = height // 2
    left = pltpu.make_async_copy(left_ref, trio.at[pl.ds(height, height)], sem.at[0])
    right = pltpu.make_async_copy(right_ref, trio.at[pl.ds(2 * height, height)], sem.at[1])
    own = pltpu.make_async_copy(own_ref, trio.at[pl.ds(0, height)], sem.at[2])
    for copy in (left, right, own):
        copy.start()
    left.wait()
    low = pltpu.make_async_copy(trio.at[pl.ds(height, half)], low_ref, sem.at[3])
    low.start()
    right.wait()
    high = pltpu.make_async_copy(trio.at[pl.ds(2 * height + half, half)], high_ref, sem.at[4])
    high.start()
    own.wait()
    whole = pltpu.make_async_copy(trio, trio_ref, sem.at[5])
    whole.start()
    for copy in (low, high, whole):
        copy.wait()


def relay(left, right, own, after):
    height, rows = own.shape
    return pl.pallas_call(
        relay_kernel,
        out_shape=[jax.ShapeDtypeStruct((part, rows), F32) for part in (3 * height, height // 2, height // 2)],
        in_specs=[ANY] * 4,
        out_specs=[ANY] * 3,
        scratch_shapes=[pltpu.VMEM((3 * height, rows), F32), pltpu.SemaphoreType.DMA((6,))],
        compiler_params=pltpu.CompilerParams(vmem_limit_bytes=EDGE_VMEM),
        cost_estimate=pl.CostEstimate(flops=0, bytes_accessed=5_000_000, transcendentals=0),
        name="relay",
    )(left, right, own, after)


TILE = 256
COEFFS_PARTS = (0, 1)
UPDATE_PARTS = (0, 0.5, 1)
BY_ROWS = (((1,), (1,)), ((), ()))


def spans(rows, parts):
    tiles = rows // TILE
    cuts = [round(tiles * part) * TILE for part in parts]
    return [(start, stop - start) for start, stop in zip(cuts, cuts[1:])]


def stacked3(left, right, dims=(((1,), (0,)), ((), ()))):
    (left_high, left_low), (right_high, right_low) = left, right
    rows = left_high.shape[0]
    both = dot(jnp.concatenate([left_high, left_low], axis=0), right_high, dims)
    return both[:rows] + both[rows:] + dot(left_high, right_low, dims)


def panel_places(height):
    at_x, at_core = lax.axis_index("x"), lax.axis_index("core")
    places = []
    for parts in (((0, 0), (-1, 0), (1, 0)), ((2, 0),), ((2, height // 2),)):
        for twin in (0, 1):
            for shift, skip in parts:
                col = lax.rem(at_x + 4 + shift, 4) * 2 + lax.rem(at_core + twin, 2)
                places.append(col * height + skip)
    return places


def coeffs_kernel(shares, width, x_ref, t_ref, *refs):
    *pieces, out_ref, panel_ref, t, panel, t_sem, sem = refs
    total = x_ref.shape[0]
    half = width // 2
    t_load = pltpu.make_async_copy(t_ref, t, t_sem.at[0])
    t_load.start()
    parts = spans(x_ref.shape[0], COEFFS_PARTS)
    height = 2 * pieces[-1].shape[0]
    places = panel_places(height)
    loads = []
    for number, (start, length) in enumerate(parts):
        span = pl.ds(start, length)
        copies = []
        for piece in pieces:
            step = min(height, piece.shape[0])
            for at in range(0, piece.shape[0], step):
                rows = pl.ds(pl.multiple_of(places[len(copies)], step), step)
                copies.append(
                    pltpu.make_async_copy(
                        piece.at[pl.ds(at, step), span], panel.at[rows, span], sem.at[number, len(copies)]
                    )
                )
        loads.append(copies)
    for copies in loads:
        for copy in copies:
            copy.start()
    coeffs = gram = None
    stores = []
    t_load.wait()
    for i in range(2):
        beside = panel_ref.at[pl.ds(i * width, width), pl.ds(total, width)]
        stores.append(pltpu.make_async_copy(t.at[i], beside, t_sem.at[i]))
        stores[-1].start()
    for number, ((start, length), copies) in enumerate(zip(parts, loads)):
        for copy in copies:
            copy.wait()
        span = pl.ds(start, length)
        stores.append(pltpu.make_async_copy(panel.at[:, span], panel_ref.at[:, span], sem.at[number, 10]))
        stores[-1].start()
        span = slice(start, start + length)
        high, low = split(panel[:, span])
        part = stacked3((high, low), split(x_ref[span, :]))
        mine = split(panel[pl.ds(pl.multiple_of(lax.axis_index("core") * half, half), half), span])
        gram_part = stacked3((high[width:], low[width:]), mine, BY_ROWS)
        coeffs = part if coeffs is None else coeffs + part
        gram = gram_part if gram is None else gram + gram_part
    a = 2 * width // shares
    out_ref[:, :a, :] = coeffs[:, :half].reshape(shares, a, half)
    out_ref[:, a : 2 * a, :] = coeffs[:, half:].reshape(shares, a, half)
    out_ref[:, 2 * a :, :] = gram.reshape(shares, width // shares, half)
    for copy in stores:
        copy.wait()


def panel_coeffs(shares, x, t, pieces):
    width = t.shape[1]
    return pl.pallas_call(
        functools.partial(coeffs_kernel, shares, width),
        out_shape=[
            jax.ShapeDtypeStruct((shares, 5 * width // shares, width // 2), F32),
            jax.ShapeDtypeStruct((2 * width, x.shape[0] + width), F32),
        ],
        in_specs=[VMEM_SPEC] + [ANY] * (1 + len(pieces)),
        out_specs=[VMEM_SPEC, ANY],
        scratch_shapes=[
            pltpu.VMEM(t.shape, F32),
            pltpu.VMEM((2 * width, x.shape[0]), F32),
            pltpu.SemaphoreType.DMA((2,)),
            pltpu.SemaphoreType.DMA((len(COEFFS_PARTS) - 1, 11)),
        ],
        compiler_params=pltpu.CompilerParams(vmem_limit_bytes=COEFFS_VMEM),
        cost_estimate=pl.CostEstimate(flops=4_000_000_000, bytes_accessed=11_000_000, transcendentals=0),
        name="panel_coeffs",
    )(x, t, *pieces)


def update_kernel(width, sums_ref, x_ref, panel_ref, twin_ref, out_ref, panel, stage, twin, t_sem, twin_sem, sem):
    rows = stage.shape[0]
    parts = spans(rows, UPDATE_PARTS)
    span = pl.ds(rows, width)
    t_load = pltpu.make_async_copy(panel_ref.at[:, span], panel.at[:, span], t_sem)
    t_load.start()
    a = 2 * width // sums_ref.shape[0]
    twin_load = pltpu.make_async_copy(twin_ref.at[:, pl.ds(2 * a, a // 2)], twin, twin_sem)
    twin_load.start()
    loads = []
    for number, (start, length) in enumerate(parts):
        span = pl.ds(start, length)
        loads.append(pltpu.make_async_copy(panel_ref.at[:, span], panel.at[:, span], sem.at[0, number]))
        loads[-1].start()
    half = width // 2
    whole = [sums_ref[:, i * a : (i + 1) * a, :].reshape(2 * width, half) for i in range(2)]
    coeffs = jnp.concatenate(whole, axis=1)
    t_load.wait()
    t = panel[:, rows:]
    first = dot3(split(t[:width]), split(coeffs[:width]))
    twin_load.wait()
    mine, other = sums_ref[:, 2 * a :, :].reshape(width, half), twin[...].reshape(width, half)
    is_first = lax.axis_index("core") == 0
    gram = jnp.concatenate([jnp.where(is_first, mine, other), jnp.where(is_first, other, mine)], axis=1)
    rest = coeffs[width:] - dot3(split(gram), split(first))
    second = dot3(split(t[width:]), split(rest))
    right = split(jnp.concatenate([first, second], axis=0))
    stores = []
    for number, (start, length) in enumerate(parts):
        loads[number].wait()
        for at in range(start, start + length, TILE):
            span = slice(at, at + TILE)
            high, low = split(panel[:, span])
            stage[span, :] = x_ref[span, :] - stacked3((high.T, low.T), right)
        span = pl.ds(start, length)
        stores.append(pltpu.make_async_copy(stage.at[span], out_ref.at[span], sem.at[1, number]))
        stores[-1].start()
    for copy in stores:
        copy.wait()


def update(sums, x, panel, twin, width):
    return pl.pallas_call(
        functools.partial(update_kernel, width),
        out_shape=jax.ShapeDtypeStruct(x.shape, F32),
        in_specs=[VMEM_SPEC, VMEM_SPEC, ANY, ANY],
        out_specs=ANY,
        scratch_shapes=[
            pltpu.VMEM(panel.shape, F32),
            pltpu.VMEM(x.shape, F32),
            pltpu.VMEM((sums.shape[0], width // sums.shape[0], width // 2), F32),
            pltpu.SemaphoreType.DMA,
            pltpu.SemaphoreType.DMA,
            pltpu.SemaphoreType.DMA((2, len(UPDATE_PARTS) - 1)),
        ],
        compiler_params=pltpu.CompilerParams(vmem_limit_bytes=UPDATE_VMEM),
        cost_estimate=pl.CostEstimate(flops=3_000_000_000, bytes_accessed=14_000_000, transcendentals=0),
        name="update",
    )(sums, x, panel, twin)


def send(value, axis, steps):
    count = lax.axis_size(axis)
    return lax.ppermute(value, axis, [(i, (i + steps) % count) for i in range(count)])


def per_device(eigvecs, reflect_y, reflect_w, panel_v, panel_t):
    rows = ("z", "y")
    shares = lax.axis_size(rows)
    own = panel_v.T

    from_left = send(own, "x", 1)
    from_right = send(own, "x", -1)
    for_below, for_above = edges(None, 0, eigvecs, reflect_y, reflect_w)
    above, below = send(for_below, rows, 1), send(for_above, rows, -1)

    x = interior(0, eigvecs, reflect_y, reflect_w)
    x, for_below, for_above = edges(0, 4, x, reflect_y, reflect_w, (above, below))
    trio, low, high = relay(from_left, from_right, own, for_below)
    low, high = send(low, "x", 1), send(high, "x", -1)
    above, below = send(for_below, rows, 1), send(for_above, rows, -1)
    twin_trio = send(trio, "core", 1)

    x = interior(4, x, reflect_y, reflect_w)
    x, low, high, above, below = lax.optimization_barrier((x, low, high, above, below))
    twin_low, twin_high = send(low, "core", 1), send(high, "core", 1)
    (x,) = edges(4, None, x, reflect_y, reflect_w, (above, below))

    pieces = [trio, twin_trio, low, twin_low, high, twin_high]
    sums, panel = panel_coeffs(shares, x, panel_t, pieces)
    mine = jnp.sum(lax.all_to_all(sums, rows, 0, 0), axis=0)
    sums = lax.all_to_all(jnp.broadcast_to(mine[None], sums.shape), rows, 0, 0)
    return update(sums, x, panel, send(sums, "core", 1), panel_t.shape[1])


def solution(mesh):
    z, y, x, core = 8, 4, 4, 2
    fine = Mesh(mesh.devices.reshape(z, y, x, core), ("z", "y", "x", "core"))
    row, col = ("z", "y"), ("x", "core")
    return jax.shard_map(
        per_device,
        mesh=fine,
        in_specs=(
            P(row, col),
            P(None, row, None, None),
            P(None, row, None, None),
            P(row, col),
            P(),
        ),
        out_specs=P(row, col),
        check_vma=False,
    )
```
